128 devices in a mesh: row: 8 (over x, core), col: 16 (over y, z).
Axes of the slice: x: 4, y: 4, z: 4, core: 2. Of those that a mesh axis runs over, the one named last changes fastest.
Arguments:
- state: float32 [180, 131072], P(None, ('row', 'col')), may hold values from -6 to 6
- neighbours: int32 [4, 131072], P(None, ('row', 'col')), may hold values from 0 to 6143
- send_faces: int32 [4, 65536], P(None, ('row', 'col')), may hold values from 0 to 4095
- jacobian: float32 [131072], P(('row', 'col')), may hold values from 0.5 to 2
- face_extract: float32 [4, 90, 180], replicated, may hold values from -0.4375 to 0.4375
- volume_op: float32 [180, 180], replicated, may hold values from -0.4375 to 0.4375
- flux_matrix: float32 [90, 90], replicated, may hold values from -0.625 to 0.625
- lift_op: float32 [180, 4, 90], replicated, may hold values from -0.3125 to 0.3125
- sf_face: int32 [32768], P(('row', 'col')), may hold values from 0 to 4095
- sf_dest: int32 [32768, 1], P(('row', 'col')), may hold values from 0 to 127, as said below
- sf_row: int32 [32768], P(('row', 'col')), may hold values from 0 to 508
- sf_col: int32 [32768], P(('row', 'col')), may hold values from 0 to 508
- sf_weights: float32 [16, 10, 32768], P(None, None, ('row', 'col')), may hold values from 0 to 0.3
- ocean: float32 [3, 4096, 8192], P(None, 'row', 'col'), may hold values from -6 to 6
- depth: float32 [4096, 8192], P('row', 'col'), may hold values from 0.5 to 2
- wet: int32 [4096, 8192], P('row', 'col'), may hold values 0 or 1
Outputs:
- state_out: float32 [180, 131072], P(None, ('row', 'col'))
- ocean_out: float32 [3, 4096, 8192], P(None, 'row', 'col')
The draws below stay inside these ranges and needn't reach their ends.
Inputs may be any that keep to these rules, and one draw needn't show every extreme that they name: `neighbours`: entries below 4096 name a face of the same partition; entry 4096 + j * 512 + k names the k-th trace received from neighbour j. `send_faces`: local face indices of the partition that holds the column. `sf_face`: local face index on the partition that holds the seafloor face. `sf_dest`: tile index r * 16 + c; each names the partition's own tile or one of the up to eight tiles beside it, diagonals included; among the seafloor faces of one partition the own tile is named exactly 64 times and no tile more than 64 times.
All inputs are finite; a program needn't handle non-finite values. No bound on the sum of `wet` on one device may be relied on, other than what follows from the above.
Results may differ from the reference program's by a relative error of at most 0.0001.
Values sent between devices are 32-bit elements; how exact they have to be, the bound alone decides.
No kernel may reach another device: no remote copies, remote signals or barrier semaphores. Data moves between devices by JAX's collectives and lax.ppermute only.
A program may use at most 128 MiB of HBM per device.

```python
import math
import jax
import jax.numpy as jnp
from jax import lax

COMPS = 9
NODES = 20
FNODES = 10
PATCH = 4
ELEM_DEV = 1024
SEND = 512
SF_DEV = 256
CY = 512
CX = 512
CAP = 64
ELEMENTS = 131072
SEAFLOOR = 32768
NY = 4096
NX = 8192
N_ROW = 8
N_COL = 16


def draw_sf_dest(key, part):
    key = jax.random.fold_in(key, 11)
    first_key = jax.random.fold_in(key, 1)
    second_key = jax.random.fold_in(key, 2)
    ndev = N_ROW * N_COL
    dev = jnp.arange(ndev, dtype=jnp.int32)
    my_row = dev // N_COL
    my_col = dev % N_COL
    slots = jnp.arange(8 * CAP, dtype=jnp.int32)
    which = slots // CAP
    offset = which + (which >= 4).astype(jnp.int32)
    near_row = my_row[:, None] + (offset // 3 - 1)[None, :]
    near_col = my_col[:, None] + (offset % 3 - 1)[None, :]
    valid = (near_row >= 0) & (near_row < N_ROW) & (near_col >= 0) & (near_col < N_COL)
    score = jax.random.randint(first_key, (ndev, 8 * CAP), 0, 65536) * (8 * CAP) + slots[None, :]
    score = score + jnp.where(valid, 0, 1 << 26)
    order = jnp.argsort(score, axis=1, stable=True)[:, :3 * CAP]
    pick_row = jnp.take_along_axis(near_row, order, axis=1)
    pick_col = jnp.take_along_axis(near_col, order, axis=1)
    own = jnp.broadcast_to((my_row * N_COL + my_col)[:, None], (ndev, CAP))
    tiles = jnp.concatenate([own, pick_row * N_COL + pick_col], axis=1)
    places = jnp.arange(SF_DEV, dtype=jnp.int32)
    mixing = jax.random.randint(second_key, (ndev, SF_DEV), 0, 65536) * SF_DEV + places[None, :]
    shuffle = jnp.argsort(mixing, axis=1, stable=True)
    tiles = jnp.take_along_axis(tiles, shuffle, axis=1)
    return tiles.reshape(-1, 1).astype(jnp.int32)


def plant(drawn, key, least, top_value):
    spot = [jax.random.randint(jax.random.fold_in(key, axis), (), 0, length) for axis, length in enumerate(drawn.shape)]
    main_axis = drawn.shape.index(max(drawn.shape))
    next_to = spot[:main_axis] + [(spot[main_axis] + 1) % drawn.shape[main_axis]] + spot[main_axis + 1:]
    return drawn.at[tuple(spot)].set(least).at[tuple(next_to)].set(top_value)


def block_levels(key, dims, cuts, least, high):
    loudness = 1.0
    for axis_at, blocks in cuts:
        heights = jax.random.uniform(jax.random.fold_in(jax.random.fold_in(key, 6), axis_at), (blocks,), jnp.float32, least / len(cuts), high / len(cuts))
        loudness = loudness * jnp.repeat(jnp.exp(heights), dims[axis_at] // blocks).reshape((-1,) + (1,) * (len(dims) - 1 - axis_at))
    return loudness


def normal_values(own_key, dims, deviation, limit, cuts=(), held_as=jnp.bfloat16):
    values = deviation * jax.random.normal(own_key, dims, jnp.float32)
    if cuts:
        values = values * block_levels(own_key, dims, cuts, -0.22, 0.18)
    return jnp.clip(values, -limit, limit).astype(held_as)


def setup_inputs(seed: int = 0) -> dict:
    splits = jax.random.split(jax.random.key(seed), 17)
    state = normal_values(splits[0], (COMPS * NODES, ELEMENTS), 1.0, 6.0, ((1, 128),), jnp.float32)
    neighbours = plant(jax.random.randint(splits[1], (4, ELEMENTS), 0, 4 * ELEM_DEV + 4 * SEND), jax.random.fold_in(splits[1], 1), 0, (4 * ELEM_DEV + 4 * SEND) - 1).astype(jnp.int32)
    send_faces = plant(jax.random.randint(splits[2], (4, SEND * N_ROW * N_COL), 0, 4 * ELEM_DEV), jax.random.fold_in(splits[2], 1), 0, (4 * ELEM_DEV) - 1).astype(jnp.int32)
    jacobian = jnp.clip(jnp.exp(math.log(2.0) - 1.3862944 * jax.random.uniform(splits[3], (ELEMENTS,), jnp.float32) ** block_levels(splits[3], (ELEMENTS,), ((0, 128),), -0.2, 0.2)), 0.5, 2.0)
    face_extract = normal_values(splits[4], (4, COMPS * FNODES, COMPS * NODES), (COMPS * NODES) ** -0.5, 0.4375, (), jnp.float32)
    volume_op = normal_values(splits[5], (COMPS * NODES, COMPS * NODES), (COMPS * NODES) ** -0.5, 0.4375, (), jnp.float32)
    flux_matrix = normal_values(splits[6], (COMPS * FNODES, COMPS * FNODES), (COMPS * FNODES) ** -0.5, 0.625, (), jnp.float32)
    lift_op = normal_values(splits[7], (COMPS * NODES, 4, COMPS * FNODES), (4 * COMPS * FNODES) ** -0.5, 0.3125, (), jnp.float32)
    sf_face = plant(jax.random.randint(splits[8], (SEAFLOOR,), 0, 4 * ELEM_DEV), jax.random.fold_in(splits[8], 1), 0, (4 * ELEM_DEV) - 1).astype(jnp.int32)
    sf_dest = draw_sf_dest(jax.random.fold_in(splits[16], 71), 0)
    sf_row = plant(jax.random.randint(splits[10], (SEAFLOOR,), 0, CY - PATCH + 1), jax.random.fold_in(splits[10], 1), 0, CY - PATCH).astype(jnp.int32)
    sf_col = plant(jax.random.randint(splits[11], (SEAFLOOR,), 0, CX - PATCH + 1), jax.random.fold_in(splits[11], 1), 0, CX - PATCH).astype(jnp.int32)
    sf_weights = jnp.clip(0.3 * jax.random.uniform(splits[12], (PATCH * PATCH, FNODES, SEAFLOOR), jnp.float32) ** block_levels(splits[12], (PATCH * PATCH, FNODES, SEAFLOOR), ((2, 128),), -0.2, 0.2), 0.0, 0.3)
    ocean = normal_values(splits[13], (3, NY, NX), 1.0, 6.0, ((1, 8), (2, 16)), jnp.float32)
    depth = jnp.clip(jnp.exp(math.log(2.0) - 1.3862944 * jax.random.uniform(splits[14], (NY, NX), jnp.float32) ** block_levels(splits[14], (NY, NX), ((0, 8), (1, 16)), -0.2, 0.2)), 0.5, 2.0)
    wet = plant((jax.random.randint(splits[15], (NY, NX), 0, 8) < 7).astype(jnp.int32), jax.random.fold_in(splits[15], 1), 0, 1)
    return dict(state=state, neighbours=neighbours, send_faces=send_faces, jacobian=jacobian, face_extract=face_extract, volume_op=volume_op, flux_matrix=flux_matrix, lift_op=lift_op, sf_face=sf_face, sf_dest=sf_dest, sf_row=sf_row, sf_col=sf_col, sf_weights=sf_weights, ocean=ocean, depth=depth, wet=wet)


HI = lax.Precision.HIGHEST


def traces_of(face_extract, q):
    t = jnp.einsum("fpk,ke->pfe", face_extract, q, precision=HI)
    return t.reshape(t.shape[0], -1)


def elastic_step(state, neighbours, send_faces, jacobian, face_extract, volume_op, flux_matrix, lift_op):
    ndev = N_ROW * N_COL
    nq = state.shape[0]
    nf = face_extract.shape[1]
    per = state.reshape(nq, ndev, ELEM_DEV).transpose(1, 0, 2)
    nb_idx = neighbours.reshape(4, ndev, ELEM_DEV).transpose(1, 0, 2).reshape(ndev, 4 * ELEM_DEV)
    sent = send_faces.reshape(4, ndev, SEND).transpose(1, 0, 2).reshape(ndev, 4 * SEND)
    jac = jacobian.reshape(ndev, ELEM_DEV)

    def publish(args):
        q, idx = args
        return jnp.take(traces_of(face_extract, q), idx, axis=1)

    parts = lax.map(publish, (per, sent)).reshape(N_ROW, N_COL, nf, 4, SEND)
    zero_row = jnp.zeros_like(parts[:1, :, :, 0])
    zero_col = jnp.zeros_like(parts[:, :1, :, 0])
    from_up = jnp.concatenate([zero_row, parts[:-1, :, :, 1]], axis=0)
    from_down = jnp.concatenate([parts[1:, :, :, 0], zero_row], axis=0)
    from_west = jnp.concatenate([zero_col, parts[:, :-1, :, 3]], axis=1)
    from_east = jnp.concatenate([parts[:, 1:, :, 2], zero_col], axis=1)
    received = jnp.concatenate([from_up, from_down, from_west, from_east], axis=3).reshape(ndev, nf, 4 * SEND)

    def update(args):
        q, idx, recv, jac_d = args
        pool = traces_of(face_extract, q)
        whole = jnp.concatenate([pool, recv], axis=1)
        near = jnp.take(whole, idx, axis=1)
        flux = jnp.dot(flux_matrix, pool - near, precision=HI).reshape(nf, 4, ELEM_DEV)
        lifted = jnp.einsum("kfq,qfe->ke", lift_op, flux, precision=HI)
        inner = jnp.dot(volume_op, q, precision=HI)
        return q + 0.25 * jac_d * (inner + lifted)

    new = lax.map(update, (per, nb_idx, received, jac))
    return new.transpose(1, 0, 2).reshape(nq, -1)


def reference(state, neighbours, send_faces, jacobian, face_extract, volume_op, flux_matrix, lift_op,
              sf_face, sf_dest, sf_row, sf_col, sf_weights, ocean, depth, wet):
    for step in range(2):
        state = elastic_step(state, neighbours, send_faces, jacobian, face_extract, volume_op, flux_matrix, lift_op)
    ndev = N_ROW * N_COL
    local = sf_face.reshape(ndev, SF_DEV)
    owner = jnp.arange(ndev, dtype=jnp.int32)[:, None]
    elem_global = (owner * ELEM_DEV + local % ELEM_DEV).reshape(-1)
    face = (local // ELEM_DEV).reshape(-1)
    chosen = jnp.take(state, elem_global, axis=1)
    vz_ops = face_extract[:, 2 * FNODES:3 * FNODES, :]
    all_faces = jnp.einsum("fpk,ks->fps", vz_ops, chosen, precision=HI)
    onehot = (face[None, :] == jnp.arange(4, dtype=jnp.int32)[:, None]).astype(jnp.float32)
    vz = jnp.sum(all_faces * onehot[:, None, :], axis=0)
    values = jnp.sum(sf_weights * vz[None], axis=1)
    dest = sf_dest[:, 0]
    cell = jnp.arange(PATCH * PATCH, dtype=jnp.int32)
    rows = (dest // N_COL) * CY + sf_row
    cols = (dest % N_COL) * CX + sf_col
    target = (rows[None, :] + (cell // PATCH)[:, None]) * NX + cols[None, :] + (cell % PATCH)[:, None]
    uplift = jnp.zeros((NY * NX,), jnp.float32).at[target.reshape(-1)].add(values.reshape(-1)).reshape(NY, NX)
    wet_f = wet.astype(jnp.float32)
    fields = ocean * wet_f[None]
    padded = jnp.pad(fields, ((0, 0), (1, 1), (1, 1)))
    north = padded[:, :-2, 1:-1]
    south = padded[:, 2:, 1:-1]
    west = padded[:, 1:-1, :-2]
    east = padded[:, 1:-1, 2:]
    avg = 0.25 * (north + south + west + east)
    height = avg[0] - 0.2 * ((east[1] - west[1]) + (south[2] - north[2])) + uplift
    speed_u = avg[1] - 0.2 * depth * (east[0] - west[0])
    speed_v = avg[2] - 0.2 * depth * (south[0] - north[0])
    ocean_out = jnp.stack([height, speed_u, speed_v]) * wet_f[None]
    return state, ocean_out
```

```python
import functools

import jax
import jax.numpy as jnp
from jax import lax
from jax.experimental import pallas as pl
from jax.experimental.pallas import tpu as pltpu
from jax.sharding import PartitionSpec as P

N_ROW = 8
N_COL = 16
ELEMS = 1024
NQ = 180
NF = 90
SEND = 512
LANES = 128
POOL = 4 * ELEMS
WHOLE = POOL + 4 * SEND
TILE = 512
EDGE = 16
BLOCK = SEND + EDGE
SF = 256
CAP = 64
GROUP = 256

F32 = jnp.float32
BF16 = jnp.bfloat16
VMEM = pl.BlockSpec(memory_space=pltpu.VMEM)
SMEM = pl.BlockSpec(memory_space=pltpu.SMEM)
NN = (((1,), (0,)), ((), ()))
NT = (((1,), (1,)), ((), ()))
TT = (((0,), (1,)), ((), ()))

PAIR_A = [(i, i ^ 1) for i in range(N_ROW)]
PAIR_B = [(i, (((i + 1) ^ 1) - 1) % N_ROW) for i in range(N_ROW)]
PAIR_C = [(i, i ^ 1) for i in range(N_COL)]
PAIR_D = [(i, (((i + 1) ^ 1) - 1) % N_COL) for i in range(N_COL)]


def call(kernel, outs, name, n_in, smem=(), scratch=(), aliases=None, flops=0):
    return pl.pallas_call(
        kernel,
        out_shape=[jax.ShapeDtypeStruct(s, d) for s, d in outs],
        in_specs=[SMEM if i in smem else VMEM for i in range(n_in)],
        out_specs=[VMEM] * len(outs),
        scratch_shapes=list(scratch),
        input_output_aliases=aliases or {},
        compiler_params=pltpu.CompilerParams(vmem_limit_bytes=40 * 2**20),
        cost_estimate=pl.CostEstimate(flops=flops, bytes_accessed=2**21, transcendentals=0),
        name=name,
    )


def split(x):
    hi = x.astype(BF16)
    return hi, (x - hi.astype(F32)).astype(BF16)


def dot(a, b, dims=NN):
    return lax.dot_general(a, b, dims, preferred_element_type=F32)


def dot3(a, b, dims=NN):
    ah, al = a
    bh, bl = b
    return dot(ah, bh, dims) + (dot(ah, bl, dims) + dot(al, bh, dims))


def parities():
    row = lax.axis_index("row")
    col = lax.axis_index("col")
    return row, col, row % 2, col % 2


def slots():
    _, _, odd_row, odd_col = parities()
    return 1 - odd_row, odd_row, 3 - odd_col, 2 + odd_col


def fill_trace_ops(extract, eh, el):
    eh[...] = jnp.zeros(eh.shape, BF16)
    el[...] = jnp.zeros(el.shape, BF16)
    for f in range(4):
        h, l = split(extract[f])
        eh[pl.ds(f * LANES, NF), :] = h
        el[pl.ds(f * LANES, NF), :] = l


def write_traces(q, eh, el, table):
    traces = dot3(split(q), (eh[...], el[...]), TT)
    for f in range(4):
        table[pl.ds(f * ELEMS, ELEMS), :] = traces[:, f * LANES : (f + 1) * LANES]


def gather_rows(index, table, out, rows):
    unroll = 16

    def step(j, carry):
        for u in range(unroll):
            at = pl.multiple_of((j * unroll + u) * 8, 8)
            got = [table[pl.ds(index(at + t), 1), :] for t in range(8)]
            out[pl.ds(at, 8), :] = jnp.concatenate(got, axis=0)
        return carry

    lax.fori_loop(0, rows // 8 // unroll, step, 0)


def gather_sends(send, table, outs):
    for slot, out in zip(slots(), outs):
        gather_rows(lambda i, slot=slot: send[slot, i], table, out, SEND)


def first_kernel(state, extract, send, table, out_a, out_b, out_c, out_d, eh, el):
    fill_trace_ops(extract, eh, el)
    write_traces(state[...], eh, el, table)
    gather_sends(send, table, (out_a, out_b, out_c, out_d))


def operators_kernel(extract, volume, flux, lift, v2, l2):
    total = volume[...]
    fl = split(flux[...])
    l2[...] = jnp.zeros(l2.shape, F32)
    for f in range(4):
        folded = dot3(split(lift[:, f, :]), fl)
        l2[:, pl.ds(f * LANES, NF)] = folded
        total = total + dot3(split(folded), split(extract[f]))
    v2[...] = total


def place_received(table, recv):
    row, col, _, _ = parities()
    gone_b = (row == 0) | (row == N_ROW - 1)
    gone_d = (col == 0) | (col == N_COL - 1)
    for slot, got, gone in zip(slots(), recv, (None, gone_b, None, gone_d)):
        value = got[pl.ds(0, SEND), :]
        if gone is not None:
            value = jnp.where(gone, 0.0, value)
        table[pl.ds(pl.multiple_of(POOL + slot * SEND, SEND), SEND), :] = value


def advance(q, near, jac, v2, l2):
    inner = dot3(split(v2), split(q))
    gathered = jnp.concatenate([near[pl.ds(f * ELEMS, ELEMS), :] for f in range(4)], axis=1)
    gathered = jnp.where(lax.broadcasted_iota(jnp.int32, gathered.shape, 1) % LANES < NF, gathered, 0.0)
    lifted = dot3(split(l2), split(gathered), NT)
    return q + 0.25 * jac * (inner - lifted)


def middle_kernel(
    state, jac, extract, v2, l2, nbr, send, table_in, in_a, in_b, in_c, in_d,
    new_state, table, out_a, out_b, out_c, out_d, eh, el, near,
):
    place_received(table, (in_a, in_b, in_c, in_d))
    gather_rows(lambda i: nbr[i], table, near, POOL)
    new = advance(state[...], near, jac[...], v2[...], l2[...])
    new_state[...] = new
    fill_trace_ops(extract, eh, el)
    write_traces(new, eh, el, table)
    gather_sends(send, table, (out_a, out_b, out_c, out_d))


def last_kernel(
    state, jac, extract, v2, l2, nbr, sf_face, sf_dest, sf_row, sf_col, weights, table_in, in_a, in_b, in_c, in_d,
    new_state, table, stay, box_a, box_b, near,
):
    place_received(table, (in_a, in_b, in_c, in_d))
    gather_rows(lambda i: nbr[i], table, near, POOL)
    new = advance(state[...], near, jac[...], v2[...], l2[...])
    new_state[...] = new
    ops = jnp.concatenate([extract[f][20:30, :] for f in range(4)], axis=0)
    on_faces = dot3(split(ops), split(new))
    elem = sf_face[...] % ELEMS
    face = sf_face[...] // ELEMS
    pick = (lax.broadcasted_iota(jnp.int32, (ELEMS, SF), 0) == elem).astype(BF16)
    fh, fl = split(on_faces)
    chosen = dot(fh, pick) + dot(fl, pick)
    vz = jnp.zeros((10, SF), F32)
    for f in range(4):
        vz = vz + jnp.where(face == f, chosen[f * 10 : (f + 1) * 10, :], 0.0)
    values = jnp.concatenate(
        [jnp.sum(weights[c] * vz, axis=0, keepdims=True) for c in range(16)]
        + [sf_row[...].astype(F32), sf_col[...].astype(F32), jnp.zeros((6, SF), F32)],
        axis=0,
    )
    row, col, odd_row, odd_col = parities()
    dest = sf_dest[...]
    dr = dest // N_COL - row
    dc = dest % N_COL - col
    to_a = 1 - 2 * odd_row
    to_c = 1 - 2 * odd_col
    group_r = jnp.where(dr == 0, 0, jnp.where(dr == to_a, 1, 2))
    group_c = jnp.where(dc == 0, 0, jnp.where(dc == to_c, 1, 2))
    group = group_r * 3 + group_c
    groups = lax.broadcasted_iota(jnp.int32, (16, SF), 0)
    owners = (groups == group).astype(F32)
    before = (
        lax.broadcasted_iota(jnp.int32, (SF, SF), 0) < lax.broadcasted_iota(jnp.int32, (SF, SF), 1)
    ).astype(BF16)
    ranks = dot(owners.astype(BF16), before)
    rank = jnp.sum(ranks * owners, axis=0, keepdims=True).astype(jnp.int32)
    place = group_r * GROUP + group_c * CAP + rank
    into = (lax.broadcasted_iota(jnp.int32, (3 * GROUP, SF), 0) == place).astype(BF16)
    vh, vl = split(values)
    box = dot(vh, into, NT) + dot(vl, into, NT)
    stay[...] = box[:, :GROUP]
    box_a[...] = box[:, GROUP : 2 * GROUP]
    box_b[...] = box[:, 2 * GROUP :]


def uplift_kernel(mine, got_c, got_d, height, wet, out, cols_h, cols_l, rows):
    lane = lax.broadcasted_iota(jnp.int32, (72, LANES), 1)
    first = jnp.where(lane < CAP, mine[:, :LANES], got_c[...])
    patches = [first[24 * g : 24 * (g + 1)] for g in range(3)]
    patches += [got_d[24 * g : 24 * (g + 1), :] for g in range(3)]
    half = lax.broadcasted_iota(jnp.int32, (24, LANES), 1) < CAP
    patches = [jnp.where(half, p, 0.0) if g >= 3 else p for g, p in enumerate(patches)]
    data = jnp.concatenate(patches, axis=1)
    total = data.shape[1]
    anchor_row = data[16:17, :].astype(jnp.int32)
    anchor_col = data[17:18, :].astype(jnp.int32)
    at = lax.broadcasted_iota(jnp.int32, (TILE, total), 0)
    d_col = at - anchor_col
    d_row = at - anchor_row
    acc = jnp.zeros((TILE, TILE), F32)
    masks = [d_col == b for b in range(4)]
    for a in range(4):
        spread = jnp.zeros((TILE, total), F32)
        for b in range(4):
            spread = jnp.where(masks[b], data[4 * a + b : 4 * a + b + 1, :], spread)
        sh, sl = split(spread)
        pick = (d_row == a).astype(BF16)
        acc = acc + (dot(pick, sh, NT) + dot(pick, sl, NT))
    out[...] = height[...] + acc * wet[...].astype(F32)


def body(
    state, neighbours, send_faces, jacobian, face_extract, volume_op, flux_matrix, lift_op,
    sf_face, sf_dest, sf_row, sf_col, sf_weights, ocean, depth, wet,
):
    nbr = neighbours.reshape(POOL)
    jac = jacobian.reshape(1, ELEMS)
    block = ((SEND, LANES), F32)
    table_t = ((WHOLE, LANES), F32)
    state_t = ((NQ, ELEMS), F32)
    trace_ops = [pltpu.VMEM((4 * LANES, NQ), BF16)] * 2
    near = pltpu.VMEM((POOL, LANES), F32)

    def exchange(a, b, c, d):
        d = lax.ppermute(d, "col", PAIR_D)
        c = lax.ppermute(c, "col", PAIR_C)
        b = lax.ppermute(b, "row", PAIR_B)
        a = lax.ppermute(a, "row", PAIR_A)
        return a, b, c, d

    table, *sends = call(
        first_kernel, [table_t] + [block] * 4, "traces_first", 3, smem=(2,), scratch=trace_ops
    )(state, face_extract, send_faces)
    recv = exchange(*sends)
    v2, l2 = call(
        operators_kernel, [((NQ, NQ), F32), ((NQ, 4 * LANES), F32)], "operators", 4
    )(face_extract, volume_op, flux_matrix, lift_op)
    state, table, *sends = call(
        middle_kernel, [state_t, table_t] + [block] * 4, "step_first", 12, smem=(5, 6),
        scratch=trace_ops + [near], aliases={7: 1},
    )(state, jac, face_extract, v2, l2, nbr, send_faces, table, *recv)
    recv = exchange(*sends)
    box_t = ((24, GROUP), F32)
    state, _, stay, box_a, box_b = call(
        last_kernel, [state_t, table_t, box_t, box_t, box_t], "step_last", 16, smem=(5,),
        scratch=[near], aliases={11: 1},
    )(
        state, jac, face_extract, v2, l2, nbr, sf_face.reshape(1, SF), sf_dest.reshape(1, SF),
        sf_row.reshape(1, SF), sf_col.reshape(1, SF), sf_weights, table, *recv,
    )
    got_b = lax.ppermute(box_b, "row", PAIR_B)
    got_a = lax.ppermute(box_a, "row", PAIR_A)
    mine = jnp.concatenate([stay, got_a, got_b], axis=0)
    got_d = lax.ppermute(mine[:, LANES:], "col", PAIR_D)
    got_c = lax.ppermute(mine[:, :LANES], "col", PAIR_C)

    wet_f = wet.astype(F32)
    fields = ocean * wet_f[None]
    row, col = lax.axis_index("row"), lax.axis_index("col")
    odd_row, odd_col = row % 2 == 1, col % 2 == 1

    def edges(first, last, axis, odd, at, count, even_pairs, odd_pairs):
        near_even = lax.ppermute(jnp.where(odd, first, last), axis, even_pairs)
        near_odd = lax.ppermute(jnp.where(odd, last, first), axis, odd_pairs)
        near_odd = jnp.where((at == 0) | (at == count - 1), 0.0, near_odd)
        return jnp.where(odd, near_even, near_odd), jnp.where(odd, near_odd, near_even)

    up, down = edges(fields[:, 0, :], fields[:, -1, :], "row", odd_row, row, N_ROW, PAIR_A, PAIR_B)
    left, right = edges(fields[:, :, 0], fields[:, :, -1], "col", odd_col, col, N_COL, PAIR_C, PAIR_D)
    north = jnp.concatenate([up[:, None, :], fields[:, :-1, :]], axis=1)
    south = jnp.concatenate([fields[:, 1:, :], down[:, None, :]], axis=1)
    west = jnp.concatenate([left[:, :, None], fields[:, :, :-1]], axis=2)
    east = jnp.concatenate([fields[:, :, 1:], right[:, :, None]], axis=2)
    avg = 0.25 * (north + south + west + east)
    height = avg[0] - 0.2 * (east[1] - west[1] + (south[2] - north[2]))
    speed_u = avg[1] - 0.2 * depth * (east[0] - west[0])
    speed_v = avg[2] - 0.2 * depth * (south[0] - north[0])
    plane = call(
        uplift_kernel, [((TILE, TILE), F32)], "uplift", 5,
        scratch=[],
    ) if False else None
    (height,) = pl.pallas_call(
        functools.partial(uplift_plain),
        out_shape=[jax.ShapeDtypeStruct((TILE, TILE), F32)],
        in_specs=[VMEM] * 5,
        out_specs=[VMEM],
        compiler_params=pltpu.CompilerParams(vmem_limit_bytes=40 * 2**20),
        name="uplift",
    )(mine, got_c, got_d, height * wet_f, wet)
    ocean_out = jnp.stack([height, speed_u * wet_f, speed_v * wet_f])
    return state, ocean_out


def uplift_plain(mine, got_c, got_d, height, wet, out):
    uplift_kernel(mine, got_c, got_d, height, wet, out, None, None, None)


def solution(mesh):
    both = ("row", "col")
    return jax.shard_map(
        body,
        mesh=mesh,
        in_specs=(
            P(None, both), P(None, both), P(None, both), P(both), P(), P(), P(), P(),
            P(both), P(both, None), P(both), P(both), P(None, None, both),
            P(None, "row", "col"), P("row", "col"), P("row", "col"),
        ),
        out_specs=(P(None, both), P(None, "row", "col")),
        check_vma=False,
    )
```

```python
import jax
import jax.numpy as jnp
from jax import lax
from jax.experimental import pallas as pl
from jax.experimental.pallas import tpu as pltpu
from jax.sharding import PartitionSpec as P

N_ROW = 8
N_COL = 16
ELEMS = 1024
NQ = 180
KP = 256
NF = 90
SEND = 512
LANES = 128
POOL = 4 * ELEMS
WHOLE = POOL + 4 * SEND
TILE = 512
EDGE = 16
EDGE_LANE = 96
SF = 256
CAP = 64
GROUP = 256
CHUNK = 256

F32 = jnp.float32
BF16 = jnp.bfloat16
VMEM = pl.BlockSpec(memory_space=pltpu.VMEM)
SMEM = pl.BlockSpec(memory_space=pltpu.SMEM)
ANY = pl.BlockSpec(memory_space=pl.ANY)
NN = (((1,), (0,)), ((), ()))
NT = (((1,), (1,)), ((), ()))

PAIR_A = [(i, i ^ 1) for i in range(N_ROW)]
PAIR_B = [(i, (((i + 1) ^ 1) - 1) % N_ROW) for i in range(N_ROW)]
PAIR_C = [(i, i ^ 1) for i in range(N_COL)]
PAIR_D = [(i, (((i + 1) ^ 1) - 1) % N_COL) for i in range(N_COL)]


def call(kernel, name, ins, outs, scratch=(), aliases=None, flops=0):
    return pl.pallas_call(
        kernel,
        out_shape=[jax.ShapeDtypeStruct(s, d) for s, d, _ in outs],
        in_specs=list(ins),
        out_specs=[spec for _, _, spec in outs],
        scratch_shapes=list(scratch),
        input_output_aliases=aliases or {},
        compiler_params=pltpu.CompilerParams(vmem_limit_bytes=32 * 2**20),
        cost_estimate=pl.CostEstimate(flops=flops, bytes_accessed=2**21, transcendentals=0),
        name=name,
    )


def split(x):
    hi = x.astype(BF16)
    return hi, (x - hi.astype(F32)).astype(BF16)


def dot(a, b, dims=NN):
    return lax.dot_general(a, b, dims, preferred_element_type=F32)


def dot3(a, b, dims=NN):
    ah, al = a
    bh, bl = b
    return dot(ah, bh, dims) + (dot(ah, bl, dims) + dot(al, bh, dims))


def left_parts(x, axis):
    hi, lo = split(x)
    return jnp.concatenate([hi, hi, lo], axis=axis)


def right_parts(x, axis):
    hi, lo = split(x)
    return jnp.concatenate([hi, lo, hi], axis=axis)


def parities():
    row = lax.axis_index("row")
    col = lax.axis_index("col")
    return row, col, row % 2, col % 2


def slots():
    _, _, odd_row, odd_col = parities()
    return 1 - odd_row, odd_row, 3 - odd_col, 2 + odd_col


def gather_rows(index, base, table, out, rows):
    unroll = 16

    def step(j, carry):
        to = j * (unroll * 8)
        for u in range(unroll):
            at = pl.multiple_of(to + u * 8, 8)
            got = [table[pl.ds(index[base + at + t], 1), :] for t in range(8)]
            out[pl.ds(at, 8), :] = jnp.concatenate(got, axis=0)
        return carry

    lax.fori_loop(0, rows // 8 // unroll, step, 0)


def gather_sends(send, table, blocks, extras, outs, sems):
    where = slots()
    copies = []
    for i in (3, 2, 1, 0):
        gather_rows(send, where[i] * SEND, table, blocks[i], SEND)
        if extras is not None:
            if i >= 2:
                blocks[i][...] = blocks[i][...] + extras[i][...]
            else:
                blocks[i][pl.ds(SEND, EDGE), :] = extras[i][...]
        copy = pltpu.make_async_copy(blocks[i], outs[i], sems.at[i])
        copy.start()
        copies.append(copy)
    return copies


def pad_state(q, padded):
    padded[pl.ds(176, KP - 176), :] = jnp.zeros((KP - 176, ELEMS), F32)
    padded[pl.ds(0, NQ), :] = q


def traces_of_chunk(padded, ek, table, c):
    at = c * CHUNK
    mine = jnp.transpose(padded[:, at : at + CHUNK])
    traces = dot(left_parts(mine, 1), ek[...], NT)
    for f in range(4):
        table[pl.ds(f * ELEMS + at, CHUNK), :] = traces[:, f * LANES : (f + 1) * LANES]


def first_kernel(state, extract, send, table, ek, out_d, out_c, out_b, out_a, full, padded, ba, bb, bc, bd, sems):
    full[...] = jnp.zeros(full.shape, F32)
    for f in range(4):
        full[pl.ds(f * LANES, NF), pl.ds(0, NQ)] = extract[:, f, :]
    ek[...] = right_parts(full[...], 1)
    pad_state(state[...], padded)
    for c in range(ELEMS // CHUNK):
        traces_of_chunk(padded, ek, table, c)
    copies = gather_sends(send, table, (ba, bb, bc, bd), None, (out_a, out_b, out_c, out_d), sems)
    for copy in copies:
        copy.wait()


def prepare_kernel(
    extract, volume_h, flux_h, lift_h, ocean_h, wet_h, v2k, l2k, ea, eb, ec, ed,
    v2, l2, volume, flux, lift, sides, ends, wet_sides, wet_ends, sems,
):
    wide = TILE - LANES
    pairs = [(flux_h, flux), (lift_h, lift), (volume_h, volume)]
    for i, at in enumerate((0, TILE - 8)):
        pairs.append((ocean_h.at[:, pl.ds(at, 8), :], ends.at[i]))
        pairs.append((wet_h.at[pl.ds(at, 8), :], wet_ends.at[i]))
    for i, at in enumerate((0, wide)):
        pairs.append((ocean_h.at[:, :, pl.ds(at, LANES)], sides.at[i]))
        pairs.append((wet_h.at[:, pl.ds(at, LANES)], wet_sides.at[i]))
    copies = [pltpu.make_async_copy(src, dst, sems.at[i]) for i, (src, dst) in enumerate(pairs)]
    for copy in copies:
        copy.start()
    for copy in copies[:3]:
        copy.wait()
    total = volume[...]
    fl = split(flux[...])
    l2[...] = jnp.zeros(l2.shape, F32)
    v2[...] = jnp.zeros(v2.shape, F32)
    for f in range(4):
        folded = dot3(split(lift[:, f, :]), fl)
        l2[:, pl.ds(f * LANES, NF)] = folded
        total = total + dot3(split(folded), split(extract[:, f, :]))
    v2[:, pl.ds(0, NQ)] = total
    v2k[...] = left_parts(v2[...], 1)
    l2k[...] = left_parts(l2[...], 1)
    for copy in copies[3:]:
        copy.wait()
    _, _, odd_row, odd_col = parities()
    lane = lax.broadcasted_iota(jnp.int32, (TILE, LANES), 1)
    last = LANES - 1
    west = wet_sides[0, :, 0:1].astype(F32)
    east = wet_sides[1, :, last : last + 1].astype(F32)
    north = wet_ends[0, 0:1, :].astype(F32)
    south = wet_ends[1, 7:8, :].astype(F32)
    to_c = jnp.zeros((TILE, LANES), F32)
    to_d = jnp.zeros((TILE, LANES), F32)
    rows_a = []
    rows_b = []
    for f in range(3):
        left = sides[0, f, :, 0:1] * west
        right = sides[1, f, :, last : last + 1] * east
        to_c = jnp.where(lane == EDGE_LANE + f, jnp.where(odd_col == 1, left, right), to_c)
        to_d = jnp.where(lane == EDGE_LANE + f, jnp.where(odd_col == 1, right, left), to_d)
        top = ends[0, f, 0:1, :] * north
        bottom = ends[1, f, 7:8, :] * south
        for rows, edge in (
            (rows_a, jnp.where(odd_row == 1, top, bottom)),
            (rows_b, jnp.where(odd_row == 1, bottom, top)),
        ):
            rows += [edge[:, t * LANES : (t + 1) * LANES] for t in range(4)]
    spare = [jnp.zeros((EDGE - 12, LANES), F32)]
    ea[...] = jnp.concatenate(rows_a + spare, axis=0)
    eb[...] = jnp.concatenate(rows_b + spare, axis=0)
    ec[...] = to_c
    ed[...] = to_d


def receive(table, recv, sems):
    copies = []
    for i, slot in enumerate(slots()):
        at = pl.multiple_of(POOL + slot * SEND, SEND)
        copy = pltpu.make_async_copy(recv[i].at[pl.ds(0, SEND), :], table.at[pl.ds(at, SEND), :], sems.at[i])
        copy.start()
        copies.append(copy)
    return copies


def zero_absent(table):
    row, col, _, _ = parities()
    for gone, slot in (
        (row == 0, 0), (row == N_ROW - 1, 1), (col == 0, 2), (col == N_COL - 1, 3),
    ):
        @pl.when(gone)
        def _():
            table[pl.ds(POOL + slot * SEND, SEND), :] = jnp.zeros((SEND, LANES), F32)


def advance(q, near, jac, v2k, l2k, new):
    size = 512
    for at in range(0, ELEMS, size):
        mine = q[:, at : at + size]
        inner = dot(v2k[...], right_parts(mine, 0))
        gathered = jnp.concatenate([near[pl.ds(f * ELEMS + at, size), :] for f in range(4)], axis=1)
        lifted = dot(l2k[...], right_parts(gathered, 1), NT)
        new[:, at : at + size] = mine[:NQ] + 0.25 * jac[:, at : at + size] * (inner - lifted)


def middle_kernel(
    state, jac, ek, v2k, l2k, ea, eb, ec, ed, nbr, send, table_in, in_a, in_b, in_c, in_d,
    new_state, table, out_d, out_c, out_b, out_a,
    padded, near, ba, bb, bc, bd, sems, out_sems,
):
    arriving = receive(table, (in_a, in_b, in_c, in_d), sems)
    pad_state(state[...], padded)
    for copy in arriving:
        copy.wait()
    zero_absent(table)
    gather_rows(nbr, 0, table, near, POOL)
    advance(padded, near, jac, v2k, l2k, new_state)
    padded[pl.ds(0, NQ), :] = new_state[...]
    for c in range(ELEMS // CHUNK):
        traces_of_chunk(padded, ek, table, c)
    copies = gather_sends(
        send, table, (ba, bb, bc, bd), (ea, eb, ec, ed), (out_a, out_b, out_c, out_d), out_sems
    )
    for copy in copies:
        copy.wait()


def last_kernel(
    state, jac, extract, v2k, l2k, nbr, sf_face, sf_dest, sf_row, sf_col, weights, table_in, in_a, in_b, in_c, in_d,
    new_state, table, stay, box_a, box_b,
    padded, near, new_local, sems, out_sem,
):
    arriving = receive(table, (in_a, in_b, in_c, in_d), sems)
    pad_state(state[...], padded)
    for copy in arriving:
        copy.wait()
    zero_absent(table)
    gather_rows(nbr, 0, table, near, POOL)
    advance(padded, near, jac, v2k, l2k, new_local)
    leaving = pltpu.make_async_copy(new_local, new_state, out_sem)
    leaving.start()
    ops = jnp.concatenate([extract[20:30, f, :] for f in range(4)], axis=0)
    on_faces = dot3(split(ops), split(new_local[...]))
    elem = sf_face[...] % ELEMS
    face = sf_face[...] // ELEMS
    pick = (lax.broadcasted_iota(jnp.int32, (ELEMS, SF), 0) == elem).astype(BF16)
    fh, fl = split(on_faces)
    chosen = dot(fh, pick) + dot(fl, pick)
    vz = jnp.zeros((10, SF), F32)
    for f in range(4):
        vz = vz + jnp.where(face == f, chosen[f * 10 : (f + 1) * 10, :], 0.0)
    values = weights[0] * vz[0:1]
    for k in range(1, 10):
        values = values + weights[k] * vz[k : k + 1]
    values = jnp.concatenate(
        [values, sf_row[...].astype(F32), sf_col[...].astype(F32), jnp.zeros((6, SF), F32)], axis=0
    )
    row, col, odd_row, odd_col = parities()
    dest = sf_dest[...]
    dr = dest // N_COL - row
    dc = dest % N_COL - col
    to_a = 1 - 2 * odd_row
    to_c = 1 - 2 * odd_col
    group_r = jnp.where(dr == 0, 0, jnp.where(dr == to_a, 1, 2))
    group_c = jnp.where(dc == 0, 0, jnp.where(dc == to_c, 1, 2))
    group = group_r * 3 + group_c
    groups = lax.broadcasted_iota(jnp.int32, (16, SF), 0)
    owners = (groups == group).astype(F32)
    before = (
        lax.broadcasted_iota(jnp.int32, (SF, SF), 0) < lax.broadcasted_iota(jnp.int32, (SF, SF), 1)
    ).astype(BF16)
    ranks = dot(owners.astype(BF16), before)
    rank = jnp.sum(ranks * owners, axis=0, keepdims=True).astype(jnp.int32)
    place = group_r * GROUP + group_c * CAP + rank
    into = (lax.broadcasted_iota(jnp.int32, (3 * GROUP, SF), 0) == place).astype(BF16)
    vh, vl = split(values)
    box = dot(vh, into, NT) + dot(vl, into, NT)
    stay[...] = box[:, :GROUP]
    box_a[...] = box[:, GROUP : 2 * GROUP]
    box_b[...] = box[:, 2 * GROUP :]
    leaving.wait()


def stencil_kernel(ocean, wet, depth, after, height, speeds, fields):
    wet_f = wet[...].astype(F32)
    for f in range(3):
        fields[f, pl.ds(0, 8), :] = jnp.zeros((8, TILE), F32)
        fields[f, pl.ds(TILE + 8, 8), :] = jnp.zeros((8, TILE), F32)
        fields[f, pl.ds(8, TILE), :] = ocean[f] * wet_f
    rows = 32
    lane = lax.broadcasted_iota(jnp.int32, (rows, TILE), 1)

    def step(i, carry):
        at = pl.multiple_of(i * rows, rows)
        mask = wet[pl.ds(at, rows), :].astype(F32)
        sums, across, along = [], [], []
        for f in range(3):
            big = fields[f, pl.ds(at, rows + 16), :]
            mine = big[8 : 8 + rows]
            up = big[7 : 7 + rows]
            down = big[9 : 9 + rows]
            west = jnp.where(lane == 0, 0.0, pltpu.roll(mine, 1, 1))
            east = jnp.where(lane == TILE - 1, 0.0, pltpu.roll(mine, TILE - 1, 1))
            sums.append(0.25 * ((up + down) + (west + east)))
            across.append(east - west)
            along.append(down - up)
        d = 0.2 * depth[pl.ds(at, rows), :]
        height[pl.ds(at, rows), :] = (sums[0] - 0.2 * (across[1] + along[2])) * mask
        speeds[0, pl.ds(at, rows), :] = (sums[1] - d * across[0]) * mask
        speeds[1, pl.ds(at, rows), :] = (sums[2] - d * along[0]) * mask
        return carry

    lax.fori_loop(0, TILE // rows, step, 0)


def add_edges(height, speeds, wet, depth, ga, gb, gc, gd):
    row, col, odd_row, odd_col = parities()
    gone_b = (row == 0) | (row == N_ROW - 1)
    gone_d = (col == 0) | (col == N_COL - 1)

    def edge_row(got, f):
        return jnp.concatenate([got[pl.ds(4 * f + t, 1), :] for t in range(4)], axis=1)

    from_a = [edge_row(ga, f) for f in range(3)]
    from_b = [jnp.where(gone_b, 0.0, edge_row(gb, f)) for f in range(3)]
    for at, sign, odd in ((0, 1.0, 1), (TILE - 1, -1.0, 0)):
        h, u, v = [jnp.where(odd_row == odd, x, y) for x, y in zip(from_a, from_b)]
        here = pl.ds(at, 1)
        mask = wet[here, :].astype(F32)
        d = (sign * 0.2) * depth[here, :]
        height[here, :] = height[here, :] + mask * (0.25 * h + (sign * 0.2) * v)
        speeds[0, here, :] = speeds[0, here, :] + mask * (0.25 * u)
        speeds[1, here, :] = speeds[1, here, :] + mask * (0.25 * v + d * h)
    lane = lax.broadcasted_iota(jnp.int32, (TILE, LANES), 1)
    from_c = [gc[:, EDGE_LANE + f : EDGE_LANE + f + 1] for f in range(3)]
    from_d = [jnp.where(gone_d, 0.0, gd[:, EDGE_LANE + f : EDGE_LANE + f + 1]) for f in range(3)]
    for at, edge, sign, odd in ((0, 0, 1.0, 1), (TILE - LANES, LANES - 1, -1.0, 0)):
        h, u, v = [jnp.where(odd_col == odd, x, y) for x, y in zip(from_c, from_d)]
        here = pl.ds(at, LANES)
        mask = jnp.where(lane == edge, wet[:, here].astype(F32), 0.0)
        d = (sign * 0.2) * depth[:, here]
        height[:, here] = height[:, here] + mask * (0.25 * h + (sign * 0.2) * u)
        speeds[0, :, here] = speeds[0, :, here] + mask * (0.25 * u + d * h)
        speeds[1, :, here] = speeds[1, :, here] + mask * (0.25 * v)


def uplift_of(data):
    total = data.shape[1]
    at = lax.broadcasted_iota(jnp.int32, (TILE, total), 0)
    d_row = at - data[16:17, :].astype(jnp.int32)
    d_col = at - data[17:18, :].astype(jnp.int32)
    masks = [d_col == b for b in range(4)]
    added = None
    for a in range(4):
        spread = jnp.zeros((TILE, total), F32)
        for b in range(4):
            spread = jnp.where(masks[b], data[4 * a + b : 4 * a + b + 1, :], spread)
        pick = (d_row == a).astype(BF16)
        part = dot(jnp.concatenate([pick, pick], axis=1), jnp.concatenate(split(spread), axis=1), NT)
        added = part if added is None else added + part
    return added


def finish_own_kernel(
    mine, wet, depth, height_in, speeds_in, in_a, in_b, in_c, in_d, height, speeds, out,
    ga, gb, gc, gd, sems, out_sem,
):
    arriving = [
        pltpu.make_async_copy(in_a.at[pl.ds(SEND, EDGE), :], ga, sems.at[0]),
        pltpu.make_async_copy(in_b.at[pl.ds(SEND, EDGE), :], gb, sems.at[1]),
        pltpu.make_async_copy(in_c, gc, sems.at[2]),
        pltpu.make_async_copy(in_d, gd, sems.at[3]),
    ]
    for copy in arriving:
        copy.start()
    for copy in arriving:
        copy.wait()
    add_edges(height, speeds, wet, depth, ga, gb, gc, gd)
    leaving = pltpu.make_async_copy(speeds, out.at[pl.ds(1, 2)], out_sem)
    leaving.start()
    half = lax.broadcasted_iota(jnp.int32, (24, LANES), 1) < CAP
    first = jnp.where(half, mine[pl.ds(0, 24), :], pltpu.roll(mine[pl.ds(24, 24), :], CAP, 1))
    second = jnp.where(half, mine[pl.ds(48, 24), :], 0.0)
    added = uplift_of(jnp.concatenate([first, second], axis=1))
    height[...] = height[...] + added * wet[...].astype(F32)
    leaving.wait()


def uplift_kernel(got_c, got_d, height, wet, whole, out, plane, sems):
    half = lax.broadcasted_iota(jnp.int32, (24, LANES), 1) < CAP
    added = uplift_of(jnp.concatenate(
        [jnp.where(half, got_d[pl.ds(24 * g, 24), :], got_c[pl.ds(24 * g, 24), :]) for g in range(3)], axis=1
    ))
    size = 128
    copies = []
    for part in range(TILE // size):
        at = part * size
        plane[pl.ds(at, size), :] = (
            height[pl.ds(at, size), :] + added[at : at + size] * wet[pl.ds(at, size), :].astype(F32)
        )
        copy = pltpu.make_async_copy(plane.at[pl.ds(at, size), :], out.at[0, pl.ds(at, size), :], sems.at[part])
        copy.start()
        copies.append(copy)
    for copy in copies:
        copy.wait()


def exchange(a, b, c, d):
    d = lax.ppermute(d, "col", PAIR_D)
    c = lax.ppermute(c, "col", PAIR_C)
    b = lax.ppermute(b, "row", PAIR_B)
    a = lax.ppermute(a, "row", PAIR_A)
    return a, b, c, d


def body(
    state, neighbours, send_faces, jacobian, face_extract, volume_op, flux_matrix, lift_op,
    sf_face, sf_dest, sf_row, sf_col, sf_weights, ocean, depth, wet,
):
    nbr = neighbours.reshape(POOL)
    send = send_faces.reshape(4 * SEND)
    jac = jacobian.reshape(1, ELEMS)
    extract = face_extract.transpose(1, 0, 2)
    weights = sf_weights.transpose(1, 0, 2)
    dma = pltpu.SemaphoreType.DMA
    short = (SEND, LANES)
    tall = (SEND + EDGE, LANES)
    table_o = ((WHOLE, LANES), F32, VMEM)
    padded = pltpu.VMEM((KP, ELEMS), F32)
    near = pltpu.VMEM((POOL, LANES), F32)

    table, ek, sd, sc, sb, sa = call(
        first_kernel, "traces_first", [VMEM, VMEM, SMEM],
        [table_o, ((4 * LANES, 3 * KP), BF16, VMEM)] + [(short, F32, ANY)] * 4,
        [pltpu.VMEM((4 * LANES, KP), F32), padded] + [pltpu.VMEM(short, F32)] * 4 + [dma((4,))], flops=10**10,
    )(state, extract, send)
    recv = exchange(sa, sb, sc, sd)
    v2k, l2k, ea, eb, ec, ed = call(
        prepare_kernel, "prepare", [VMEM] + [pl.BlockSpec(memory_space=pltpu.HBM)] * 5,
        [((NQ, 3 * KP), BF16, VMEM), ((NQ, 12 * LANES), BF16, VMEM)]
        + [((EDGE, LANES), F32, VMEM)] * 2 + [(short, F32, VMEM)] * 2,
        [
            pltpu.VMEM((NQ, KP), F32), pltpu.VMEM((NQ, 4 * LANES), F32), pltpu.VMEM((NQ, NQ), F32),
            pltpu.VMEM((NF, NF), F32), pltpu.VMEM((NQ, 4, NF), F32), pltpu.VMEM((2, 3, TILE, LANES), F32),
            pltpu.VMEM((2, 3, 8, TILE), F32), pltpu.VMEM((2, TILE, LANES), jnp.int32),
            pltpu.VMEM((2, 8, TILE), jnp.int32), dma((11,)),
        ], flops=5*10**9,
    )(extract, volume_op, flux_matrix, lift_op, ocean, wet)
    state, table, sd, sc, sb, sa = call(
        middle_kernel, "step_first", [VMEM] * 9 + [SMEM] * 2 + [VMEM] + [ANY] * 4,
        [((NQ, ELEMS), F32, VMEM), table_o] + [(short, F32, ANY)] * 2 + [(tall, F32, ANY)] * 2,
        [padded, near] + [pltpu.VMEM(tall, F32)] * 2 + [pltpu.VMEM(short, F32)] * 2 + [dma((4,)), dma((4,))],
        aliases={11: 1},
    )(state, jac, ek, v2k, l2k, ea, eb, ec, ed, nbr, send, table, *recv)
    recv = exchange(sa, sb, sc, sd)
    height, speeds = call(
        stencil_kernel, "stencil", [VMEM] * 4,
        [((TILE, TILE), F32, VMEM), ((2, TILE, TILE), F32, VMEM)],
        [pltpu.VMEM((3, TILE + 16, TILE), F32)], flops=10**9,
    )(ocean, wet, depth, state[:8, :LANES])
    box_o = ((24, GROUP), F32, VMEM)
    state, _, stay, box_a, box_b = call(
        last_kernel, "step_last", [VMEM] * 5 + [SMEM] + [VMEM] * 6 + [ANY] * 4,
        [((NQ, ELEMS), F32, ANY), table_o, box_o, box_o, box_o],
        [padded, near, pltpu.VMEM((NQ, ELEMS), F32), dma((4,)), dma(())],
        aliases={11: 1},
    )(
        state, jac, extract, v2k, l2k, nbr, sf_face.reshape(1, SF), sf_dest.reshape(1, SF),
        sf_row.reshape(1, SF), sf_col.reshape(1, SF), weights, table, *recv,
    )
    got_b = lax.ppermute(box_b, "row", PAIR_B)
    got_a = lax.ppermute(box_a, "row", PAIR_A)
    mine = jnp.concatenate([stay, got_a, got_b], axis=0)
    own = mine[:, :LANES]
    height, _, ocean_out = call(
        finish_own_kernel, "finish_own", [VMEM] * 5 + [ANY] * 4,
        [((TILE, TILE), F32, VMEM), ((2, TILE, TILE), F32, VMEM), ((3, TILE, TILE), F32, ANY)],
        [pltpu.VMEM((EDGE, LANES), F32)] * 2 + [pltpu.VMEM(short, F32)] * 2 + [dma((4,)), dma(())],
        aliases={3: 0, 4: 1}, flops=10**9,
    )(own, wet, depth, height, speeds, *recv)
    got_d = lax.ppermute(mine[:, LANES:], "col", PAIR_D)
    got_c = lax.ppermute(own, "col", PAIR_C)
    (ocean_out,) = call(
        uplift_kernel, "uplift", [VMEM] * 4 + [ANY], [((3, TILE, TILE), F32, ANY)],
        [pltpu.VMEM((TILE, TILE), F32), dma((4,))],
        aliases={4: 0},
    )(got_c, got_d, height, wet, ocean_out)
    return state, ocean_out


def solution(mesh):
    both = ("row", "col")
    return jax.shard_map(
        body,
        mesh=mesh,
        in_specs=(
            P(None, both), P(None, both), P(None, both), P(both), P(), P(), P(), P(),
            P(both), P(both, None), P(both), P(both), P(None, None, both),
            P(None, "row", "col"), P("row", "col"), P("row", "col"),
        ),
        out_specs=(P(None, both), P(None, "row", "col")),
        check_vma=False,
    )
```

```python
import jax
import jax.numpy as jnp
from jax import lax
from jax.experimental import pallas as pl
from jax.experimental.pallas import tpu as pltpu
from jax.sharding import PartitionSpec as P

N_ROW = 8
N_COL = 16
ELEMS = 1024
NQ = 180
KP = 256
NF = 90
SEND = 512
LANES = 128
POOL = 4 * ELEMS
WHOLE = POOL + 4 * SEND
TILE = 512
EDGE = 16
EDGE_LANE = 96
SF = 256
CAP = 64
GROUP = 256
CHUNK = 256
SIZE = 256

F32 = jnp.float32
BF16 = jnp.bfloat16
VMEM = pl.BlockSpec(memory_space=pltpu.VMEM)
SMEM = pl.BlockSpec(memory_space=pltpu.SMEM)
ANY = pl.BlockSpec(memory_space=pl.ANY)
NN = (((1,), (0,)), ((), ()))
NT = (((1,), (1,)), ((), ()))

BOTH = ("row", "col")


def at(r, c):
    return r * N_COL + c


def pairs_of(partner):
    return [(at(r, c), at(*partner(r, c))) for r in range(N_ROW) for c in range(N_COL)]


def step_out(i):
    return i + 1 if i % 2 else i - 1


PAIR_A = pairs_of(lambda r, c: (r ^ 1, c))
PAIR_B = pairs_of(lambda r, c: (step_out(r), c) if 0 < r < N_ROW - 1 else ((r, c ^ 4) if c % 4 in (1, 2) else (N_ROW - 1 - r, c)))
PAIR_C = pairs_of(lambda r, c: (r, c ^ 1))
PAIR_D = pairs_of(lambda r, c: (r, step_out(c)) if 0 < c < N_COL - 1 else (r ^ 1, c))


def call(kernel, name, ins, outs, scratch=(), aliases=None, flops=0):
    return pl.pallas_call(
        kernel,
        out_shape=[jax.ShapeDtypeStruct(s, d) for s, d, _ in outs],
        in_specs=list(ins),
        out_specs=[spec for _, _, spec in outs],
        scratch_shapes=list(scratch),
        input_output_aliases=aliases or {},
        compiler_params=pltpu.CompilerParams(vmem_limit_bytes=32 * 2**20),
        cost_estimate=pl.CostEstimate(flops=flops, bytes_accessed=2**21, transcendentals=0),
        name=name,
    )


def split(x):
    hi = x.astype(BF16)
    return hi, (x - hi.astype(F32)).astype(BF16)


def dot(a, b, dims=NN):
    return lax.dot_general(a, b, dims, preferred_element_type=F32)


def dot3(a, b, dims=NN):
    ah, al = a
    bh, bl = b
    return dot(ah, bh, dims) + (dot(ah, bl, dims) + dot(al, bh, dims))


def left_parts(x, axis):
    hi, lo = split(x)
    return jnp.concatenate([hi, hi, lo], axis=axis)


def right_parts(x, axis):
    hi, lo = split(x)
    return jnp.concatenate([hi, lo, hi], axis=axis)


def parities():
    row = lax.axis_index("row")
    col = lax.axis_index("col")
    return row, col, row % 2, col % 2


def slots():
    _, _, odd_row, odd_col = parities()
    return 1 - odd_row, odd_row, 3 - odd_col, 2 + odd_col


def gather_rows(index, base, table, out, rows):
    unroll = 16

    def step(j, carry):
        to = j * (unroll * 8)
        for u in range(unroll):
            at = pl.multiple_of(to + u * 8, 8)
            got = [table[pl.ds(index[base + at + t], 1), :] for t in range(8)]
            out[pl.ds(at, 8), :] = jnp.concatenate(got, axis=0)
        return carry

    lax.fori_loop(0, rows // 8 // unroll, step, 0)


def gather_sends(send, table, blocks, extras, outs, sems):
    where = slots()
    copies = []
    for i in (3, 2, 1, 0):
        gather_rows(send, where[i] * SEND, table, blocks[i], SEND)
        if extras is not None:
            if i >= 2:
                blocks[i][pl.ds(0, SEND), :] = blocks[i][pl.ds(0, SEND), :] + extras[i][...]
            else:
                blocks[i][pl.ds(SEND, EDGE), :] = extras[i][...]
        copy = pltpu.make_async_copy(blocks[i], outs[i], sems.at[i])
        copy.start()
        copies.append(copy)
    return copies


def pad_state(q, padded):
    padded[pl.ds(176, KP - 176), :] = jnp.zeros((KP - 176, ELEMS), F32)
    padded[pl.ds(0, NQ), :] = q


def traces_of_chunk(padded, ek, table, c):
    at = c * CHUNK
    mine = jnp.transpose(padded[:, at : at + CHUNK])
    traces = dot(left_parts(mine, 1), ek[...], NT)
    for f in range(4):
        table[pl.ds(f * ELEMS + at, CHUNK), :] = traces[:, f * LANES : (f + 1) * LANES]


def first_kernel(state, extract, send, table, ek, out_d, out_c, out_b, out_a, full, padded, ba, bb, bc, bd, sems):
    full[...] = jnp.zeros(full.shape, F32)
    for f in range(4):
        full[pl.ds(f * LANES, NF), pl.ds(0, NQ)] = extract[:, f, :]
    ek[...] = right_parts(full[...], 1)
    pad_state(state[...], padded)
    for c in range(ELEMS // CHUNK):
        traces_of_chunk(padded, ek, table, c)
    copies = gather_sends(send, table, (ba, bb, bc, bd), None, (out_a, out_b, out_c, out_d), sems)
    for copy in copies:
        copy.wait()


def prepare_kernel(extract, volume, flux, lift, ocean, wet, v2k, l2k, ea, eb, ec, ed, v2, l2):
    total = volume[...]
    fl = split(flux[...])
    l2[...] = jnp.zeros(l2.shape, F32)
    v2[...] = jnp.zeros(v2.shape, F32)
    for f in range(4):
        folded = dot3(split(lift[:, f, :]), fl)
        l2[:, pl.ds(f * LANES, NF)] = folded
        total = total + dot3(split(folded), split(extract[:, f, :]))
    v2[:, pl.ds(0, NQ)] = total
    v2k[...] = left_parts(v2[...], 1)
    l2k[...] = left_parts(l2[...], 1)
    _, _, odd_row, odd_col = parities()
    lane = lax.broadcasted_iota(jnp.int32, (TILE, LANES), 1)
    west = wet[:, 0:1].astype(F32)
    east = wet[:, TILE - 1 : TILE].astype(F32)
    north = wet[0:1, :].astype(F32)
    south = wet[TILE - 1 : TILE, :].astype(F32)
    to_c = jnp.zeros((TILE, LANES), F32)
    to_d = jnp.zeros((TILE, LANES), F32)
    rows_a = []
    rows_b = []
    for f in range(3):
        left = ocean[f, :, 0:1] * west
        right = ocean[f, :, TILE - 1 : TILE] * east
        to_c = jnp.where(lane == EDGE_LANE + f, jnp.where(odd_col == 1, left, right), to_c)
        to_d = jnp.where(lane == EDGE_LANE + f, jnp.where(odd_col == 1, right, left), to_d)
        top = ocean[f, 0:1, :] * north
        bottom = ocean[f, TILE - 1 : TILE, :] * south
        for rows, edge in (
            (rows_a, jnp.where(odd_row == 1, top, bottom)),
            (rows_b, jnp.where(odd_row == 1, bottom, top)),
        ):
            rows += [edge[:, t * LANES : (t + 1) * LANES] for t in range(4)]
    spare = [jnp.zeros((EDGE - 12, LANES), F32)]
    ea[...] = jnp.concatenate(rows_a + spare, axis=0)
    eb[...] = jnp.concatenate(rows_b + spare, axis=0)
    ec[...] = to_c
    ed[...] = to_d


def receive(table, recv, sems):
    copies = []
    for i, slot in enumerate(slots()):
        at = pl.multiple_of(POOL + slot * SEND, SEND)
        copy = pltpu.make_async_copy(recv[i].at[pl.ds(0, SEND), :], table.at[pl.ds(at, SEND), :], sems.at[i])
        copy.start()
        copies.append(copy)
    return copies


def zero_absent(table):
    row, col, _, _ = parities()
    for gone, slot in (
        (row == 0, 0), (row == N_ROW - 1, 1), (col == 0, 2), (col == N_COL - 1, 3),
    ):
        @pl.when(gone)
        def _():
            table[pl.ds(POOL + slot * SEND, SEND), :] = jnp.zeros((SEND, LANES), F32)


def gather_part(index, table, near, at):
    for f in range(4):
        for u in range(0, SIZE, 8):
            got = [table[pl.ds(index[f * ELEMS + at + u + t], 1), :] for t in range(8)]
            near[pl.ds(f * SIZE + u, 8), :] = jnp.concatenate(got, axis=0)


def advance_part(q, near, jac, v2k, l2k, at):
    here = pl.ds(at, SIZE)
    mine = q[:, here]
    inner = dot(v2k[...], right_parts(mine, 0))
    gathered = jnp.concatenate([near[pl.ds(f * SIZE, SIZE), :] for f in range(4)], axis=1)
    lifted = dot(l2k[...], right_parts(gathered, 1), NT)
    return mine[:NQ] + 0.25 * jac[:, here] * (inner - lifted)


def sweep(index, table, near0, near1, work):
    pairs = ELEMS // SIZE // 2
    gather_part(index, table, near0, 0)

    def step(i, carry):
        at = pl.multiple_of(i * (2 * SIZE), 2 * SIZE)
        gather_part(index, table, near1, at + SIZE)
        work(near0, at)
        gather_part(index, table, near0, at + 2 * SIZE)
        work(near1, at + SIZE)
        return carry

    lax.fori_loop(0, pairs - 1, step, 0)
    at = ELEMS - 2 * SIZE
    gather_part(index, table, near1, at + SIZE)
    work(near0, at)
    work(near1, at + SIZE)


def middle_kernel(
    state, jac, ek, v2k, l2k, ea, eb, ec, ed, nbr, send, table_in, in_d, in_c, in_b, in_a,
    new_state, table, out_d, out_c, out_b, out_a,
    padded, near0, near1, ba, bb, bc, bd, sems, out_sems,
):
    arriving = receive(table, (in_a, in_b, in_c, in_d), sems)
    pad_state(state[...], padded)
    for copy in arriving:
        copy.wait()
    zero_absent(table)

    def work(near, at):
        new_state[:, pl.ds(at, SIZE)] = advance_part(padded, near, jac, v2k, l2k, at)

    sweep(nbr, table, near0, near1, work)
    padded[pl.ds(0, NQ), :] = new_state[...]
    for c in range(ELEMS // CHUNK):
        traces_of_chunk(padded, ek, table, c)
    copies = gather_sends(
        send, table, (ba, bb, bc, bd), (ea, eb, ec, ed), (out_a, out_b, out_c, out_d), out_sems
    )
    for copy in copies:
        copy.wait()


def last_kernel(
    state, jac, extract, v2k, l2k, nbr, sf_face, sf_dest, sf_row, sf_col, weights, table_in, in_d, in_c, in_b, in_a,
    new_state, table, stay, box_a, box_b,
    padded, near0, near1, new_local, sems, out_sem,
):
    arriving = receive(table, (in_a, in_b, in_c, in_d), sems)
    pad_state(state[...], padded)
    for copy in arriving:
        copy.wait()
    zero_absent(table)

    def work(near, at):
        new_local[:, pl.ds(at, SIZE)] = advance_part(padded, near, jac, v2k, l2k, at)

    sweep(nbr, table, near0, near1, work)
    leaving = pltpu.make_async_copy(new_local, new_state, out_sem)
    leaving.start()
    ops = jnp.concatenate([extract[20:30, f, :] for f in range(4)], axis=0)
    on_faces = dot3(split(ops), split(new_local[...]))
    elem = sf_face[...] % ELEMS
    face = sf_face[...] // ELEMS
    pick = (lax.broadcasted_iota(jnp.int32, (ELEMS, SF), 0) == elem).astype(BF16)
    fh, fl = split(on_faces)
    chosen = dot(fh, pick) + dot(fl, pick)
    vz = jnp.zeros((10, SF), F32)
    for f in range(4):
        vz = vz + jnp.where(face == f, chosen[f * 10 : (f + 1) * 10, :], 0.0)
    values = weights[0] * vz[0:1]
    for k in range(1, 10):
        values = values + weights[k] * vz[k : k + 1]
    values = jnp.concatenate(
        [values, sf_row[...].astype(F32), sf_col[...].astype(F32), jnp.zeros((6, SF), F32)], axis=0
    )
    row, col, odd_row, odd_col = parities()
    dest = sf_dest[...]
    dr = dest // N_COL - row
    dc = dest % N_COL - col
    to_a = 1 - 2 * odd_row
    to_c = 1 - 2 * odd_col
    group_r = jnp.where(dr == 0, 0, jnp.where(dr == to_a, 1, 2))
    group_c = jnp.where(dc == 0, 0, jnp.where(dc == to_c, 1, 2))
    group = group_r * 3 + group_c
    groups = lax.broadcasted_iota(jnp.int32, (16, SF), 0)
    owners = (groups == group).astype(F32)
    before = (
        lax.broadcasted_iota(jnp.int32, (SF, SF), 0) < lax.broadcasted_iota(jnp.int32, (SF, SF), 1)
    ).astype(BF16)
    ranks = dot(owners.astype(BF16), before)
    rank = jnp.sum(ranks * owners, axis=0, keepdims=True).astype(jnp.int32)
    place = group_r * GROUP + group_c * CAP + rank
    into = (lax.broadcasted_iota(jnp.int32, (3 * GROUP, SF), 0) == place).astype(BF16)
    vh, vl = split(values)
    box = dot(vh, into, NT) + dot(vl, into, NT)
    stay[...] = box[:, :GROUP]
    box_a[...] = box[:, GROUP : 2 * GROUP]
    box_b[...] = box[:, 2 * GROUP :]
    leaving.wait()


def stencil_kernel(ocean, wet, depth, after, height, speeds, fields):
    wet_f = wet[...].astype(F32)
    for f in range(3):
        fields[f, pl.ds(0, 8), :] = jnp.zeros((8, TILE), F32)
        fields[f, pl.ds(TILE + 8, 8), :] = jnp.zeros((8, TILE), F32)
        fields[f, pl.ds(8, TILE), :] = ocean[f] * wet_f
    rows = 32
    lane = lax.broadcasted_iota(jnp.int32, (rows, TILE), 1)

    def step(i, carry):
        at = pl.multiple_of(i * rows, rows)
        mask = wet[pl.ds(at, rows), :].astype(F32)
        sums, across, along = [], [], []
        for f in range(3):
            big = fields[f, pl.ds(at, rows + 16), :]
            mine = big[8 : 8 + rows]
            up = big[7 : 7 + rows]
            down = big[9 : 9 + rows]
            west = jnp.where(lane == 0, 0.0, pltpu.roll(mine, 1, 1))
            east = jnp.where(lane == TILE - 1, 0.0, pltpu.roll(mine, TILE - 1, 1))
            sums.append(0.25 * ((up + down) + (west + east)))
            across.append(east - west)
            along.append(down - up)
        d = 0.2 * depth[pl.ds(at, rows), :]
        height[pl.ds(at, rows), :] = (sums[0] - 0.2 * (across[1] + along[2])) * mask
        speeds[0, pl.ds(at, rows), :] = (sums[1] - d * across[0]) * mask
        speeds[1, pl.ds(at, rows), :] = (sums[2] - d * along[0]) * mask
        return carry

    lax.fori_loop(0, TILE // rows, step, 0)


def add_edges(height, speeds, wet, depth, ga, gb, gc, gd):
    row, col, odd_row, odd_col = parities()
    gone_b = (row == 0) | (row == N_ROW - 1)
    gone_d = (col == 0) | (col == N_COL - 1)

    def edge_row(got, f):
        return jnp.concatenate([got[pl.ds(4 * f + t, 1), :] for t in range(4)], axis=1)

    from_a = [edge_row(ga, f) for f in range(3)]
    from_b = [jnp.where(gone_b, 0.0, edge_row(gb, f)) for f in range(3)]
    for at, sign, odd in ((0, 1.0, 1), (TILE - 1, -1.0, 0)):
        h, u, v = [jnp.where(odd_row == odd, x, y) for x, y in zip(from_a, from_b)]
        here = pl.ds(at, 1)
        mask = wet[here, :].astype(F32)
        d = (sign * 0.2) * depth[here, :]
        height[here, :] = height[here, :] + mask * (0.25 * h + (sign * 0.2) * v)
        speeds[0, here, :] = speeds[0, here, :] + mask * (0.25 * u)
        speeds[1, here, :] = speeds[1, here, :] + mask * (0.25 * v + d * h)
    lane = lax.broadcasted_iota(jnp.int32, (TILE, LANES), 1)
    from_c = [gc[:, EDGE_LANE + f : EDGE_LANE + f + 1] for f in range(3)]
    from_d = [jnp.where(gone_d, 0.0, gd[:, EDGE_LANE + f : EDGE_LANE + f + 1]) for f in range(3)]
    for at, edge, sign, odd in ((0, 0, 1.0, 1), (TILE - LANES, LANES - 1, -1.0, 0)):
        h, u, v = [jnp.where(odd_col == odd, x, y) for x, y in zip(from_c, from_d)]
        here = pl.ds(at, LANES)
        mask = jnp.where(lane == edge, wet[:, here].astype(F32), 0.0)
        d = (sign * 0.2) * depth[:, here]
        height[:, here] = height[:, here] + mask * (0.25 * h + (sign * 0.2) * u)
        speeds[0, :, here] = speeds[0, :, here] + mask * (0.25 * u + d * h)
        speeds[1, :, here] = speeds[1, :, here] + mask * (0.25 * v)


def uplift_of(data):
    total = data.shape[1]
    at = lax.broadcasted_iota(jnp.int32, (TILE, total), 0)
    d_row = at - data[16:17, :].astype(jnp.int32)
    d_col = at - data[17:18, :].astype(jnp.int32)
    masks = [d_col == b for b in range(4)]
    added = None
    for a in range(4):
        spread = jnp.zeros((TILE, total), F32)
        for b in range(4):
            spread = jnp.where(masks[b], data[4 * a + b : 4 * a + b + 1, :], spread)
        pick = (d_row == a).astype(BF16)
        part = dot(jnp.concatenate([pick, pick], axis=1), jnp.concatenate(split(spread), axis=1), NT)
        added = part if added is None else added + part
    return added


def finish_own_kernel(
    mine, wet, depth, height_in, speeds_in, in_d, in_c, in_b, in_a, height, speeds, out,
    ga, gb, gc, gd, sems, out_sem,
):
    arriving = [
        pltpu.make_async_copy(in_a.at[pl.ds(SEND, EDGE), :], ga, sems.at[0]),
        pltpu.make_async_copy(in_b.at[pl.ds(SEND, EDGE), :], gb, sems.at[1]),
        pltpu.make_async_copy(in_c.at[pl.ds(0, SEND), :], gc, sems.at[2]),
        pltpu.make_async_copy(in_d.at[pl.ds(0, SEND), :], gd, sems.at[3]),
    ]
    for copy in arriving:
        copy.start()
    for copy in arriving:
        copy.wait()
    add_edges(height, speeds, wet, depth, ga, gb, gc, gd)
    leaving = pltpu.make_async_copy(speeds, out.at[pl.ds(1, 2)], out_sem)
    leaving.start()
    half = lax.broadcasted_iota(jnp.int32, (24, LANES), 1) < CAP
    first = jnp.where(half, mine[pl.ds(0, 24), :], pltpu.roll(mine[pl.ds(24, 24), :], CAP, 1))
    second = jnp.where(half, mine[pl.ds(48, 24), :], 0.0)
    added = uplift_of(jnp.concatenate([first, second], axis=1))
    height[...] = height[...] + added * wet[...].astype(F32)
    leaving.wait()


def uplift_kernel(got_d, got_c, height, wet, whole, out, plane, sems):
    half = lax.broadcasted_iota(jnp.int32, (24, LANES), 1) < CAP
    added = uplift_of(jnp.concatenate(
        [jnp.where(half, got_d[pl.ds(24 * g, 24), :], got_c[pl.ds(24 * g, 24), :]) for g in range(3)], axis=1
    ))
    size = 128
    copies = []
    for part in range(TILE // size):
        at = part * size
        plane[pl.ds(at, size), :] = (
            height[pl.ds(at, size), :] + added[at : at + size] * wet[pl.ds(at, size), :].astype(F32)
        )
        copy = pltpu.make_async_copy(plane.at[pl.ds(at, size), :], out.at[0, pl.ds(at, size), :], sems.at[part])
        copy.start()
        copies.append(copy)
    for copy in copies:
        copy.wait()


def exchange(a, b, c, d):
    d = lax.ppermute(d, BOTH, PAIR_D)
    c = lax.ppermute(c, BOTH, PAIR_C)
    b = lax.ppermute(b, BOTH, PAIR_B)
    a = lax.ppermute(a, BOTH, PAIR_A)
    return d, c, b, a


def body(
    state, neighbours, send_faces, jacobian, face_extract, volume_op, flux_matrix, lift_op,
    sf_face, sf_dest, sf_row, sf_col, sf_weights, ocean, depth, wet,
):
    nbr = neighbours.reshape(POOL)
    send = send_faces.reshape(4 * SEND)
    jac = jacobian.reshape(1, ELEMS)
    extract = face_extract.transpose(1, 0, 2)
    weights = sf_weights.transpose(1, 0, 2)
    dma = pltpu.SemaphoreType.DMA
    short = (SEND, LANES)
    tall = (SEND + EDGE, LANES)
    table_o = ((WHOLE, LANES), F32, VMEM)
    padded = pltpu.VMEM((KP, ELEMS), F32)
    near = [pltpu.VMEM((4 * SIZE, LANES), F32)] * 2

    table, ek, sd, sc, sb, sa = call(
        first_kernel, "traces_first", [VMEM, VMEM, SMEM],
        [table_o, ((4 * LANES, 3 * KP), BF16, VMEM)] + [(short, F32, ANY)] * 4,
        [pltpu.VMEM((4 * LANES, KP), F32), padded] + [pltpu.VMEM(short, F32)] * 4 + [dma((4,))], flops=10**10,
    )(state, extract, send)
    recv = exchange(sa, sb, sc, sd)
    v2k, l2k, ea, eb, ec, ed = call(
        prepare_kernel, "prepare", [VMEM] * 6,
        [((NQ, 3 * KP), BF16, VMEM), ((NQ, 12 * LANES), BF16, VMEM)]
        + [((EDGE, LANES), F32, VMEM)] * 2 + [(short, F32, VMEM)] * 2,
        [pltpu.VMEM((NQ, KP), F32), pltpu.VMEM((NQ, 4 * LANES), F32)], flops=5 * 10**9,
    )(extract, volume_op, flux_matrix, lift_op, ocean, wet)
    state, table, sd, sc, sb, sa = call(
        middle_kernel, "step_first", [VMEM] * 9 + [SMEM] * 2 + [VMEM] + [ANY] * 4,
        [((NQ, ELEMS), F32, VMEM), table_o] + [(tall, F32, ANY)] * 4,
        [padded] + near + [pltpu.VMEM(tall, F32)] * 4 + [dma((4,)), dma((4,))],
        aliases={11: 1},
    )(state, jac, ek, v2k, l2k, ea, eb, ec, ed, nbr, send, table, *recv)
    recv = exchange(sa, sb, sc, sd)
    height, speeds = call(
        stencil_kernel, "stencil", [VMEM] * 4,
        [((TILE, TILE), F32, VMEM), ((2, TILE, TILE), F32, VMEM)],
        [pltpu.VMEM((3, TILE + 16, TILE), F32)], flops=10**9,
    )(ocean, wet, depth, state[:8, :LANES])
    box_o = ((24, GROUP), F32, VMEM)
    state, _, stay, box_a, box_b = call(
        last_kernel, "step_last", [VMEM] * 5 + [SMEM] + [VMEM] * 6 + [ANY] * 4,
        [((NQ, ELEMS), F32, ANY), table_o, box_o, box_o, box_o],
        [padded] + near + [pltpu.VMEM((NQ, ELEMS), F32), dma((4,)), dma(())],
        aliases={11: 1},
    )(
        state, jac, extract, v2k, l2k, nbr, sf_face.reshape(1, SF), sf_dest.reshape(1, SF),
        sf_row.reshape(1, SF), sf_col.reshape(1, SF), weights, table, *recv,
    )
    got_b = lax.ppermute(box_b, BOTH, PAIR_B)
    got_a = lax.ppermute(box_a, BOTH, PAIR_A)
    mine = jnp.concatenate([stay, got_b, got_a], axis=0)
    own = mine[:, :LANES]
    height, _, ocean_out = call(
        finish_own_kernel, "finish_own", [VMEM] * 5 + [ANY] * 4,
        [((TILE, TILE), F32, VMEM), ((2, TILE, TILE), F32, VMEM), ((3, TILE, TILE), F32, ANY)],
        [pltpu.VMEM((EDGE, LANES), F32)] * 2 + [pltpu.VMEM(short, F32)] * 2 + [dma((4,)), dma(())],
        aliases={3: 0, 4: 1}, flops=10**9,
    )(own, wet, depth, height, speeds, *recv)
    got_d = lax.ppermute(mine[:, LANES:], BOTH, PAIR_D)
    got_c = lax.ppermute(own, BOTH, PAIR_C)
    (ocean_out,) = call(
        uplift_kernel, "uplift", [VMEM] * 4 + [ANY], [((3, TILE, TILE), F32, ANY)],
        [pltpu.VMEM((TILE, TILE), F32), dma((4,))],
        aliases={4: 0}, flops=3 * 10**9,
    )(got_d, got_c, height, wet, ocean_out)
    return state, ocean_out


def solution(mesh):
    both = ("row", "col")
    return jax.shard_map(
        body,
        mesh=mesh,
        in_specs=(
            P(None, both), P(None, both), P(None, both), P(both), P(), P(), P(), P(),
            P(both), P(both, None), P(both), P(both), P(None, None, both),
            P(None, "row", "col"), P("row", "col"), P("row", "col"),
        ),
        out_specs=(P(None, both), P(None, "row", "col")),
        check_vma=False,
    )
```

```python
import jax
import jax.numpy as jnp
from jax import lax
from jax.experimental import pallas as pl
from jax.experimental.pallas import tpu as pltpu
from jax.sharding import PartitionSpec as P

N_ROW = 8
N_COL = 16
ELEMS = 1024
NQ = 180
KP = 256
NF = 90
SEND = 512
LANES = 128
POOL = 4 * ELEMS
WHOLE = POOL + 4 * SEND
TILE = 512
EDGE = 16
EDGE_LANE = 96
SF = 256
CAP = 64
GROUP = 256
CHUNK = 256
SIZE = 256

F32 = jnp.float32
BF16 = jnp.bfloat16
VMEM = pl.BlockSpec(memory_space=pltpu.VMEM)
SMEM = pl.BlockSpec(memory_space=pltpu.SMEM)
ANY = pl.BlockSpec(memory_space=pl.ANY)
NN = (((1,), (0,)), ((), ()))
NT = (((1,), (1,)), ((), ()))

BOTH = ("row", "col")


def at(r, c):
    return r * N_COL + c


def pairs_of(partner):
    return [(at(r, c), at(*partner(r, c))) for r in range(N_ROW) for c in range(N_COL)]


def step_out(i):
    return i + 1 if i % 2 else i - 1


PAIR_A = pairs_of(lambda r, c: (r ^ 1, c))
PAIR_B = pairs_of(lambda r, c: (step_out(r), c) if 0 < r < N_ROW - 1 else ((r, c ^ 4) if c % 4 in (1, 2) else (N_ROW - 1 - r, c)))
PAIR_B_SMALL = pairs_of(lambda r, c: (step_out(r), c) if 0 < r < N_ROW - 1 else (r, c ^ 1))
PAIR_C = pairs_of(lambda r, c: (r, c ^ 1))
PAIR_D = pairs_of(lambda r, c: (r, step_out(c)) if 0 < c < N_COL - 1 else (r ^ 1, c))


def call(kernel, name, ins, outs, scratch=(), aliases=None, flops=0):
    return pl.pallas_call(
        kernel,
        out_shape=[jax.ShapeDtypeStruct(s, d) for s, d, _ in outs],
        in_specs=list(ins),
        out_specs=[spec for _, _, spec in outs],
        scratch_shapes=list(scratch),
        input_output_aliases=aliases or {},
        compiler_params=pltpu.CompilerParams(vmem_limit_bytes=32 * 2**20),
        cost_estimate=pl.CostEstimate(flops=flops, bytes_accessed=2**21, transcendentals=0),
        name=name,
    )


def split(x):
    hi = x.astype(BF16)
    return hi, (x - hi.astype(F32)).astype(BF16)


def dot(a, b, dims=NN):
    return lax.dot_general(a, b, dims, preferred_element_type=F32)


def dot3(a, b, dims=NN):
    ah, al = a
    bh, bl = b
    return dot(ah, bh, dims) + (dot(ah, bl, dims) + dot(al, bh, dims))


def left_parts(x, axis):
    hi, lo = split(x)
    return jnp.concatenate([hi, hi, lo], axis=axis)


def right_parts(x, axis):
    hi, lo = split(x)
    return jnp.concatenate([hi, lo, hi], axis=axis)


def parities():
    row = lax.axis_index("row")
    col = lax.axis_index("col")
    return row, col, row % 2, col % 2


def slots():
    _, _, odd_row, odd_col = parities()
    return 1 - odd_row, odd_row, 3 - odd_col, 2 + odd_col


def gather_rows(index, which, table, out, rows):
    def step(j, carry):
        to = j * LANES
        base = j * (4 * LANES) + which * LANES
        for u in range(0, LANES, 8):
            got = [table[pl.ds(index[base + u + t], 1), :] for t in range(8)]
            out[pl.ds(pl.multiple_of(to + u, 8), 8), :] = jnp.concatenate(got, axis=0)
        return carry

    lax.fori_loop(0, rows // LANES, step, 0)


def gather_sends(send, table, blocks, extras, outs, sems):
    where = slots()
    copies = []
    for i in (3, 2, 1, 0):
        gather_rows(send, where[i], table, blocks[i], SEND)
        if extras is not None:
            if i >= 2:
                blocks[i][pl.ds(0, SEND), :] = blocks[i][pl.ds(0, SEND), :] + extras[i][...]
            else:
                blocks[i][pl.ds(SEND, EDGE), :] = extras[i][...]
        copy = pltpu.make_async_copy(blocks[i], outs[i], sems.at[i])
        copy.start()
        copies.append(copy)
    return copies


def pad_state(q, padded):
    padded[pl.ds(176, KP - 176), :] = jnp.zeros((KP - 176, ELEMS), F32)
    padded[pl.ds(0, NQ), :] = q


def traces_of_chunk(padded, ek, table, c):
    at = c * CHUNK
    mine = jnp.transpose(padded[:, at : at + CHUNK])
    traces = dot(left_parts(mine, 1), ek[...], NT)
    for f in range(4):
        table[pl.ds(f * ELEMS + at, CHUNK), :] = traces[:, f * LANES : (f + 1) * LANES]


def blank_kernel(blank):
    blank[...] = jnp.zeros(blank.shape, F32)


def first_kernel(
    state, extract, send, blank, table, ek, out_d, out_c, out_b, out_a, full, padded, ba, bb, bc, bd, sems
):
    for f in range(4):
        full[pl.ds(f * LANES, NF), pl.ds(0, NQ)] = extract[:, f, :]
    ek[...] = right_parts(full[...], 1)
    pad_state(state[...], padded)
    for c in range(ELEMS // CHUNK):
        traces_of_chunk(padded, ek, table, c)
    copies = gather_sends(send, table, (ba, bb, bc, bd), None, (out_a, out_b, out_c, out_d), sems)
    for copy in copies:
        copy.wait()


def prepare_kernel(extract, volume, flux, lift, ocean, wet, v2k, l2k, ea, eb, ec, ed, v2, l2):
    total = volume[...]
    fl = split(flux[...])
    l2[...] = jnp.zeros(l2.shape, F32)
    v2[...] = jnp.zeros(v2.shape, F32)
    for f in range(4):
        folded = dot3(split(lift[:, f, :]), fl)
        l2[:, pl.ds(f * LANES, NF)] = folded
        total = total + dot3(split(folded), split(extract[:, f, :]))
    v2[:, pl.ds(0, NQ)] = total
    v2k[...] = left_parts(v2[...], 1)
    l2k[...] = left_parts(l2[...], 1)
    _, _, odd_row, odd_col = parities()
    lane = lax.broadcasted_iota(jnp.int32, (TILE, LANES), 1)
    west = wet[:, 0:1].astype(F32)
    east = wet[:, TILE - 1 : TILE].astype(F32)
    north = wet[0:1, :].astype(F32)
    south = wet[TILE - 1 : TILE, :].astype(F32)
    to_c = jnp.zeros((TILE, LANES), F32)
    to_d = jnp.zeros((TILE, LANES), F32)
    rows_a = []
    rows_b = []
    for f in range(3):
        left = ocean[f, :, 0:1] * west
        right = ocean[f, :, TILE - 1 : TILE] * east
        to_c = jnp.where(lane == EDGE_LANE + f, jnp.where(odd_col == 1, left, right), to_c)
        to_d = jnp.where(lane == EDGE_LANE + f, jnp.where(odd_col == 1, right, left), to_d)
        top = ocean[f, 0:1, :] * north
        bottom = ocean[f, TILE - 1 : TILE, :] * south
        for rows, edge in (
            (rows_a, jnp.where(odd_row == 1, top, bottom)),
            (rows_b, jnp.where(odd_row == 1, bottom, top)),
        ):
            rows += [edge[:, t * LANES : (t + 1) * LANES] for t in range(4)]
    spare = [jnp.zeros((EDGE - 12, LANES), F32)]
    ea[...] = jnp.concatenate(rows_a + spare, axis=0)
    eb[...] = jnp.concatenate(rows_b + spare, axis=0)
    ec[...] = to_c
    ed[...] = to_d


def receive(table, recv, sems):
    copies = []
    for i, slot in enumerate(slots()):
        at = pl.multiple_of(POOL + slot * SEND, SEND)
        copy = pltpu.make_async_copy(recv[i].at[pl.ds(0, SEND), :], table.at[pl.ds(at, SEND), :], sems.at[i])
        copy.start()
        copies.append(copy)
    return copies


def zero_absent(table):
    row, col, _, _ = parities()
    for gone, slot in (
        (row == 0, 0), (row == N_ROW - 1, 1), (col == 0, 2), (col == N_COL - 1, 3),
    ):
        @pl.when(gone)
        def _():
            table[pl.ds(POOL + slot * SEND, SEND), :] = jnp.zeros((SEND, LANES), F32)


def gather_part(index, table, near, at):
    for f in range(4):
        for u in range(0, SIZE, 8):
            base = 4 * at + (u // LANES) * (4 * LANES) + f * LANES + u % LANES
            got = [table[pl.ds(index[base + t], 1), :] for t in range(8)]
            near[pl.ds(f * SIZE + u, 8), :] = jnp.concatenate(got, axis=0)


def advance_part(q, near, jac, v2k, l2k, at):
    here = pl.ds(at, SIZE)
    mine = q[:, here]
    inner = dot(v2k[...], right_parts(mine, 0))
    gathered = jnp.concatenate([near[pl.ds(f * SIZE, SIZE), :] for f in range(4)], axis=1)
    lifted = dot(l2k[...], right_parts(gathered, 1), NT)
    return mine[:NQ] + 0.25 * jac[:, here] * (inner - lifted)


def sweep(index, table, near0, near1, work):
    pairs = ELEMS // SIZE // 2
    gather_part(index, table, near0, 0)

    def step(i, carry):
        at = pl.multiple_of(i * (2 * SIZE), 2 * SIZE)
        gather_part(index, table, near1, at + SIZE)
        work(near0, at)
        gather_part(index, table, near0, at + 2 * SIZE)
        work(near1, at + SIZE)
        return carry

    lax.fori_loop(0, pairs - 1, step, 0)
    at = ELEMS - 2 * SIZE
    gather_part(index, table, near1, at + SIZE)
    work(near0, at)
    work(near1, at + SIZE)


def middle_kernel(
    state, jac, ek, v2k, l2k, ea, eb, ec, ed, nbr, send, table_in, in_d, in_c, in_b, in_a,
    new_state, table, out_d, out_c, out_b, out_a,
    padded, near0, near1, ba, bb, bc, bd, sems, out_sems,
):
    arriving = receive(table, (in_a, in_b, in_c, in_d), sems)
    pad_state(state[...], padded)
    for copy in arriving:
        copy.wait()
    zero_absent(table)

    def work(near, at):
        new_state[:, pl.ds(at, SIZE)] = advance_part(padded, near, jac, v2k, l2k, at)

    sweep(nbr, table, near0, near1, work)
    padded[pl.ds(0, NQ), :] = new_state[...]
    for c in range(ELEMS // CHUNK):
        traces_of_chunk(padded, ek, table, c)
    copies = gather_sends(
        send, table, (ba, bb, bc, bd), (ea, eb, ec, ed), (out_a, out_b, out_c, out_d), out_sems
    )
    for copy in copies:
        copy.wait()


def last_kernel(
    state, jac, extract, v2k, l2k, nbr, sf_face, pick, into, sf_row, sf_col, weights, table_in, in_d, in_c, in_b, in_a,
    new_state, table, stay, box_a, box_b,
    padded, near0, near1, new_local, sems, out_sem,
):
    arriving = receive(table, (in_a, in_b, in_c, in_d), sems)
    pad_state(state[...], padded)
    for copy in arriving:
        copy.wait()
    zero_absent(table)

    def work(near, at):
        new_local[:, pl.ds(at, SIZE)] = advance_part(padded, near, jac, v2k, l2k, at)

    sweep(nbr, table, near0, near1, work)
    leaving = pltpu.make_async_copy(new_local, new_state, out_sem)
    leaving.start()
    ops = jnp.concatenate([extract[20:30, f, :] for f in range(4)], axis=0)
    on_faces = dot3(split(ops), split(new_local[...]))
    face = sf_face[...] // ELEMS
    fh, fl = split(on_faces)
    chosen = dot(fh, pick[...]) + dot(fl, pick[...])
    vz = jnp.zeros((10, SF), F32)
    for f in range(4):
        vz = vz + jnp.where(face == f, chosen[f * 10 : (f + 1) * 10, :], 0.0)
    values = weights[0] * vz[0:1]
    for k in range(1, 10):
        values = values + weights[k] * vz[k : k + 1]
    values = jnp.concatenate(
        [values, sf_row[...].astype(F32), sf_col[...].astype(F32), jnp.zeros((6, SF), F32)], axis=0
    )
    vh, vl = split(values)
    box = dot(vh, into[...], NT) + dot(vl, into[...], NT)
    stay[...] = box[:, :GROUP]
    box_a[...] = box[:, GROUP : 2 * GROUP]
    box_b[...] = box[:, 2 * GROUP :]
    leaving.wait()


def place_faces(sf_face, sf_dest, pick, into):
    elem = sf_face[...] % ELEMS
    pick[...] = (lax.broadcasted_iota(jnp.int32, (ELEMS, SF), 0) == elem).astype(BF16)
    row, col, odd_row, odd_col = parities()
    dest = sf_dest[...]
    dr = dest // N_COL - row
    dc = dest % N_COL - col
    to_a = 1 - 2 * odd_row
    to_c = 1 - 2 * odd_col
    group_r = jnp.where(dr == 0, 0, jnp.where(dr == to_a, 1, 2))
    group_c = jnp.where(dc == 0, 0, jnp.where(dc == to_c, 1, 2))
    group = group_r * 3 + group_c
    groups = lax.broadcasted_iota(jnp.int32, (16, SF), 0)
    owners = (groups == group).astype(F32)
    before = (
        lax.broadcasted_iota(jnp.int32, (SF, SF), 0) < lax.broadcasted_iota(jnp.int32, (SF, SF), 1)
    ).astype(BF16)
    ranks = dot(owners.astype(BF16), before)
    rank = jnp.sum(ranks * owners, axis=0, keepdims=True).astype(jnp.int32)
    place = group_r * GROUP + group_c * CAP + rank
    into[...] = (lax.broadcasted_iota(jnp.int32, (3 * GROUP, SF), 0) == place).astype(BF16)


def stencil_kernel(ocean, wet, depth, sf_face, sf_dest, after, height, speeds, pick, into, fields):
    place_faces(sf_face, sf_dest, pick, into)
    wet_f = wet[...].astype(F32)
    for f in range(3):
        fields[f, pl.ds(0, 8), :] = jnp.zeros((8, TILE), F32)
        fields[f, pl.ds(TILE + 8, 8), :] = jnp.zeros((8, TILE), F32)
        fields[f, pl.ds(8, TILE), :] = ocean[f] * wet_f
    rows = 32
    lane = lax.broadcasted_iota(jnp.int32, (rows, TILE), 1)

    def step(i, carry):
        at = pl.multiple_of(i * rows, rows)
        mask = wet[pl.ds(at, rows), :].astype(F32)
        sums, across, along = [], [], []
        for f in range(3):
            big = fields[f, pl.ds(at, rows + 16), :]
            mine = big[8 : 8 + rows]
            up = big[7 : 7 + rows]
            down = big[9 : 9 + rows]
            west = jnp.where(lane == 0, 0.0, pltpu.roll(mine, 1, 1))
            east = jnp.where(lane == TILE - 1, 0.0, pltpu.roll(mine, TILE - 1, 1))
            sums.append(0.25 * ((up + down) + (west + east)))
            across.append(east - west)
            along.append(down - up)
        d = 0.2 * depth[pl.ds(at, rows), :]
        height[pl.ds(at, rows), :] = (sums[0] - 0.2 * (across[1] + along[2])) * mask
        speeds[0, pl.ds(at, rows), :] = (sums[1] - d * across[0]) * mask
        speeds[1, pl.ds(at, rows), :] = (sums[2] - d * along[0]) * mask
        return carry

    lax.fori_loop(0, TILE // rows, step, 0)


def add_edges(height, speeds, wet, depth, ga, gb, gc, gd):
    row, col, odd_row, odd_col = parities()
    gone_b = (row == 0) | (row == N_ROW - 1)
    gone_d = (col == 0) | (col == N_COL - 1)

    def edge_row(got, f):
        return jnp.concatenate([got[pl.ds(4 * f + t, 1), :] for t in range(4)], axis=1)

    from_a = [edge_row(ga, f) for f in range(3)]
    from_b = [jnp.where(gone_b, 0.0, edge_row(gb, f)) for f in range(3)]
    for at, sign, odd in ((0, 1.0, 1), (TILE - 1, -1.0, 0)):
        h, u, v = [jnp.where(odd_row == odd, x, y) for x, y in zip(from_a, from_b)]
        here = pl.ds(at, 1)
        mask = wet[here, :].astype(F32)
        d = (sign * 0.2) * depth[here, :]
        height[here, :] = height[here, :] + mask * (0.25 * h + (sign * 0.2) * v)
        speeds[0, here, :] = speeds[0, here, :] + mask * (0.25 * u)
        speeds[1, here, :] = speeds[1, here, :] + mask * (0.25 * v + d * h)
    lane = lax.broadcasted_iota(jnp.int32, (TILE, LANES), 1)
    from_c = [gc[:, EDGE_LANE + f : EDGE_LANE + f + 1] for f in range(3)]
    from_d = [jnp.where(gone_d, 0.0, gd[:, EDGE_LANE + f : EDGE_LANE + f + 1]) for f in range(3)]
    for at, edge, sign, odd in ((0, 0, 1.0, 1), (TILE - LANES, LANES - 1, -1.0, 0)):
        h, u, v = [jnp.where(odd_col == odd, x, y) for x, y in zip(from_c, from_d)]
        here = pl.ds(at, LANES)
        mask = jnp.where(lane == edge, wet[:, here].astype(F32), 0.0)
        d = (sign * 0.2) * depth[:, here]
        height[:, here] = height[:, here] + mask * (0.25 * h + (sign * 0.2) * u)
        speeds[0, :, here] = speeds[0, :, here] + mask * (0.25 * u + d * h)
        speeds[1, :, here] = speeds[1, :, here] + mask * (0.25 * v)


def uplift_of(data, first=0, columns=TILE):
    total = data.shape[1]
    d_row = lax.broadcasted_iota(jnp.int32, (TILE, total), 0) - data[16:17, :].astype(jnp.int32)
    d_col = lax.broadcasted_iota(jnp.int32, (columns, total), 0) + (first - data[17:18, :].astype(jnp.int32))
    masks = [d_col == b for b in range(4)]
    added = None
    for a in range(4):
        spread = jnp.zeros((columns, total), F32)
        for b in range(4):
            spread = jnp.where(masks[b], data[4 * a + b : 4 * a + b + 1, :], spread)
        pick = (d_row == a).astype(BF16)
        part = dot(jnp.concatenate([pick, pick], axis=1), jnp.concatenate(split(spread), axis=1), NT)
        added = part if added is None else added + part
    return added


def side_by_side(blocks, first):
    half = lax.broadcasted_iota(jnp.int32, (24, LANES), 1) < CAP

    def at_lane(x, lane):
        if x is None:
            return jnp.zeros((24, LANES), F32)
        return x if lane == first else pltpu.roll(x, CAP, 1)

    pairs = [(blocks[i], blocks[i + 1] if i + 1 < len(blocks) else None) for i in range(0, len(blocks), 2)]
    return jnp.concatenate([jnp.where(half, at_lane(x, 0), at_lane(y, CAP)) for x, y in pairs], axis=1)


def finish_edges_kernel(
    stay, wet, depth, height_in, speeds_in, in_d, in_c, in_b, in_a, height, speeds, ga, gb, gc, gd, sems,
):
    arriving = [
        pltpu.make_async_copy(in_a.at[pl.ds(SEND, EDGE), :], ga, sems.at[0]),
        pltpu.make_async_copy(in_b.at[pl.ds(SEND, EDGE), :], gb, sems.at[1]),
        pltpu.make_async_copy(in_c.at[pl.ds(0, SEND), :], gc, sems.at[2]),
        pltpu.make_async_copy(in_d.at[pl.ds(0, SEND), :], gd, sems.at[3]),
    ]
    for copy in arriving:
        copy.start()
    for copy in arriving:
        copy.wait()
    add_edges(height, speeds, wet, depth, ga, gb, gc, gd)
    added = uplift_of(side_by_side([stay[:, :LANES]], 0))
    height[...] = height[...] + added * wet[...].astype(F32)


def uplift_own_kernel(got_b, got_a, wet, height_in, speeds, height, out, out_sem):
    leaving = pltpu.make_async_copy(speeds, out.at[pl.ds(1, 2)], out_sem)
    leaving.start()
    added = uplift_of(side_by_side([got_b[:, :LANES], got_a[:, :LANES]], 0))
    height[...] = height[...] + added * wet[...].astype(F32)
    leaving.wait()


def uplift_far_kernel(got_d, got_c, wet, height, whole, out, plane, sems):
    half = lax.broadcasted_iota(jnp.int32, (24, LANES), 1) < CAP
    data = jnp.concatenate(
        [jnp.where(half, got_d[pl.ds(24 * g, 24), :], got_c[pl.ds(24 * g, 24), :]) for g in range(3)], axis=1
    )
    size = TILE // 2
    copies = []
    for part in range(2):
        here = pl.ds(part * size, size)
        added = uplift_of(data, part * size, size)
        plane[:, here] = height[:, here] + added * wet[:, here].astype(F32)
        copy = pltpu.make_async_copy(plane.at[:, here], out.at[0, :, here], sems.at[part])
        copy.start()
        copies.append(copy)
    for copy in copies:
        copy.wait()


def exchange(a, b, c, d):
    d = lax.ppermute(d, BOTH, PAIR_D)
    c = lax.ppermute(c, BOTH, PAIR_C)
    b = lax.ppermute(b, BOTH, PAIR_B)
    a = lax.ppermute(a, BOTH, PAIR_A)
    return d, c, b, a


def stored_order(index):
    return index.reshape(4, -1, LANES).transpose(1, 0, 2).reshape(-1)


def body(
    state, neighbours, send_faces, jacobian, face_extract, volume_op, flux_matrix, lift_op,
    sf_face, sf_dest, sf_row, sf_col, sf_weights, ocean, depth, wet,
):
    nbr = stored_order(neighbours)
    send = stored_order(send_faces)
    jac = jacobian.reshape(1, ELEMS)
    extract = face_extract.transpose(1, 0, 2)
    weights = sf_weights.transpose(1, 0, 2)
    dma = pltpu.SemaphoreType.DMA
    short = (SEND, LANES)
    tall = (SEND + EDGE, LANES)
    table_o = ((WHOLE, LANES), F32, VMEM)
    padded = pltpu.VMEM((KP, ELEMS), F32)
    near = [pltpu.VMEM((4 * SIZE, LANES), F32)] * 2

    blank_o = ((4 * LANES, KP), F32, VMEM)
    (blank,) = call(blank_kernel, "blank", [], [blank_o], flops=10**10)()
    table, ek, sd, sc, sb, sa, _ = call(
        first_kernel, "traces_first", [VMEM, VMEM, SMEM, VMEM],
        [table_o, ((4 * LANES, 3 * KP), BF16, VMEM)] + [(short, F32, ANY)] * 4 + [blank_o],
        [padded] + [pltpu.VMEM(short, F32)] * 4 + [dma((4,))], aliases={3: 6}, flops=10**10,
    )(state, extract, send, blank)
    recv = exchange(sa, sb, sc, sd)
    v2k, l2k, ea, eb, ec, ed = call(
        prepare_kernel, "prepare", [VMEM] * 6,
        [((NQ, 3 * KP), BF16, VMEM), ((NQ, 12 * LANES), BF16, VMEM)]
        + [((EDGE, LANES), F32, VMEM)] * 2 + [(short, F32, VMEM)] * 2,
        [pltpu.VMEM((NQ, KP), F32), pltpu.VMEM((NQ, 4 * LANES), F32)], flops=5 * 10**9,
    )(extract, volume_op, flux_matrix, lift_op, ocean, wet)
    state, table, sd, sc, sb, sa = call(
        middle_kernel, "step_first", [VMEM] * 9 + [SMEM] * 2 + [VMEM] + [ANY] * 4,
        [((NQ, ELEMS), F32, VMEM), table_o] + [(tall, F32, ANY)] * 4,
        [padded] + near + [pltpu.VMEM(tall, F32)] * 4 + [dma((4,)), dma((4,))],
        aliases={11: 1},
    )(state, jac, ek, v2k, l2k, ea, eb, ec, ed, nbr, send, table, *recv)
    recv = exchange(sa, sb, sc, sd)
    height, speeds, pick, into = call(
        stencil_kernel, "stencil", [VMEM] * 6,
        [
            ((TILE, TILE), F32, VMEM), ((2, TILE, TILE), F32, VMEM),
            ((ELEMS, SF), BF16, VMEM), ((3 * GROUP, SF), BF16, VMEM),
        ],
        [pltpu.VMEM((3, TILE + 16, TILE), F32)], flops=10**9,
    )(ocean, wet, depth, sf_face.reshape(1, SF), sf_dest.reshape(1, SF), state[:8, :LANES])
    box_o = ((24, GROUP), F32, VMEM)
    state, _, stay, box_a, box_b = call(
        last_kernel, "step_last", [VMEM] * 5 + [SMEM] + [VMEM] * 7 + [ANY] * 4,
        [((NQ, ELEMS), F32, ANY), table_o, box_o, box_o, box_o],
        [padded] + near + [pltpu.VMEM((NQ, ELEMS), F32), dma((4,)), dma(())],
        aliases={12: 1},
    )(
        state, jac, extract, v2k, l2k, nbr, sf_face.reshape(1, SF), pick, into,
        sf_row.reshape(1, SF), sf_col.reshape(1, SF), weights, table, *recv,
    )
    got_b = lax.ppermute(box_b, BOTH, PAIR_B_SMALL)
    got_a = lax.ppermute(box_a, BOTH, PAIR_A)
    plane_o = ((TILE, TILE), F32, VMEM)
    height, speeds = call(
        finish_edges_kernel, "finish_edges", [VMEM] * 5 + [ANY] * 4,
        [plane_o, ((2, TILE, TILE), F32, VMEM)],
        [pltpu.VMEM((EDGE, LANES), F32)] * 2 + [pltpu.VMEM(short, F32)] * 2 + [dma((4,))],
        aliases={3: 0, 4: 1}, flops=2 * 10**9,
    )(stay, wet, depth, height, speeds, *recv)
    mine = jnp.concatenate([stay, got_b, got_a], axis=0)
    got_d = lax.ppermute(mine[:, LANES:], BOTH, PAIR_D)
    got_c = lax.ppermute(jnp.pad(mine[:, :LANES], ((0, 8), (0, 0))), BOTH, PAIR_C)
    height, ocean_out = call(
        uplift_own_kernel, "uplift_own", [VMEM] * 5, [plane_o, ((3, TILE, TILE), F32, ANY)], [dma(())],
        aliases={3: 0}, flops=10**9,
    )(got_b, got_a, wet, height, speeds)
    (ocean_out,) = call(
        uplift_far_kernel, "uplift_far", [VMEM] * 4 + [ANY], [((3, TILE, TILE), F32, ANY)],
        [pltpu.VMEM((TILE, TILE), F32), dma((2,))], aliases={4: 0}, flops=3 * 10**9,
    )(got_d, got_c, wet, height, ocean_out)
    return state, ocean_out


def solution(mesh):
    both = ("row", "col")
    return jax.shard_map(
        body,
        mesh=mesh,
        in_specs=(
            P(None, both), P(None, both), P(None, both), P(both), P(), P(), P(), P(),
            P(both), P(both, None), P(both), P(both), P(None, None, both),
            P(None, "row", "col"), P("row", "col"), P("row", "col"),
        ),
        out_specs=(P(None, both), P(None, "row", "col")),
        check_vma=False,
    )
```

```python
import jax
import jax.numpy as jnp
from jax import lax
from jax.experimental import pallas as pl
from jax.experimental.pallas import tpu as pltpu
from jax.sharding import PartitionSpec as P

N_ROW = 8
N_COL = 16
ELEMS = 1024
NQ = 180
KP = 256
NF = 90
SEND = 512
LANES = 128
POOL = 4 * ELEMS
WHOLE = POOL + 4 * SEND
TILE = 512
EDGE = 16
EDGE_LANE = 96
SF = 256
CAP = 64
GROUP = 256
CHUNK = 256
SIZE = 256

F32 = jnp.float32
BF16 = jnp.bfloat16
VMEM = pl.BlockSpec(memory_space=pltpu.VMEM)
SMEM = pl.BlockSpec(memory_space=pltpu.SMEM)
ANY = pl.BlockSpec(memory_space=pl.ANY)
NN = (((1,), (0,)), ((), ()))
NT = (((1,), (1,)), ((), ()))

BOTH = ("row", "col")


def at(r, c):
    return r * N_COL + c


def pairs_of(partner):
    return [(at(r, c), at(*partner(r, c))) for r in range(N_ROW) for c in range(N_COL)]


def step_out(i):
    return i + 1 if i % 2 else i - 1


PAIR_A = pairs_of(lambda r, c: (r ^ 1, c))
PAIR_B = pairs_of(lambda r, c: (step_out(r), c) if 0 < r < N_ROW - 1 else ((r, c ^ 4) if c % 4 in (1, 2) else (N_ROW - 1 - r, c)))
PAIR_B_SMALL = pairs_of(lambda r, c: (step_out(r), c) if 0 < r < N_ROW - 1 else (r, c ^ 1))
PAIR_C = pairs_of(lambda r, c: (r, c ^ 1))
PAIR_D = pairs_of(lambda r, c: (r, step_out(c)) if 0 < c < N_COL - 1 else (r ^ 1, c))


def call(kernel, name, ins, outs, scratch=(), aliases=None, flops=0):
    return pl.pallas_call(
        kernel,
        out_shape=[jax.ShapeDtypeStruct(s, d) for s, d, _ in outs],
        in_specs=list(ins),
        out_specs=[spec for _, _, spec in outs],
        scratch_shapes=list(scratch),
        input_output_aliases=aliases or {},
        compiler_params=pltpu.CompilerParams(vmem_limit_bytes=32 * 2**20),
        cost_estimate=pl.CostEstimate(flops=flops, bytes_accessed=2**21, transcendentals=0),
        name=name,
    )


def split(x):
    hi = x.astype(BF16)
    return hi, (x - hi.astype(F32)).astype(BF16)


def dot(a, b, dims=NN):
    return lax.dot_general(a, b, dims, preferred_element_type=F32)


def dot3(a, b, dims=NN):
    ah, al = a
    bh, bl = b
    return dot(ah, bh, dims) + (dot(ah, bl, dims) + dot(al, bh, dims))


def left_parts(x, axis):
    hi, lo = split(x)
    return jnp.concatenate([hi, hi, lo], axis=axis)


def right_parts(x, axis):
    hi, lo = split(x)
    return jnp.concatenate([hi, lo, hi], axis=axis)


def parities():
    row = lax.axis_index("row")
    col = lax.axis_index("col")
    return row, col, row % 2, col % 2


def slots():
    _, _, odd_row, odd_col = parities()
    return 1 - odd_row, odd_row, 3 - odd_col, 2 + odd_col


def gather_rows(index, which, table, out, rows):
    def step(j, carry):
        to = j * LANES
        base = j * (4 * LANES) + which * LANES
        for u in range(0, LANES, 8):
            got = [table[pl.ds(index[base + u + t], 1), :] for t in range(8)]
            out[pl.ds(pl.multiple_of(to + u, 8), 8), :] = jnp.concatenate(got, axis=0)
        return carry

    lax.fori_loop(0, rows // LANES, step, 0)


def gather_sends(send, table, blocks, extras, outs, sems):
    where = slots()
    copies = []
    for i in (3, 2, 1, 0):
        gather_rows(send, where[i], table, blocks[i], SEND)
        if extras is not None:
            if i >= 2:
                blocks[i][pl.ds(0, SEND), :] = blocks[i][pl.ds(0, SEND), :] + extras[i][...]
            else:
                blocks[i][pl.ds(SEND, EDGE), :] = extras[i][...]
        copy = pltpu.make_async_copy(blocks[i], outs[i], sems.at[i])
        copy.start()
        copies.append(copy)
    return copies


def pad_state(q, padded):
    padded[pl.ds(176, KP - 176), :] = jnp.zeros((KP - 176, ELEMS), F32)
    padded[pl.ds(0, NQ), :] = q


def traces_of_chunk(padded, ek, table, c):
    at = c * CHUNK
    mine = jnp.transpose(padded[:, at : at + CHUNK])
    traces = dot(left_parts(mine, 1), ek[...], NT)
    for f in range(4):
        table[pl.ds(f * ELEMS + at, CHUNK), :] = traces[:, f * LANES : (f + 1) * LANES]


def blank_kernel(blank):
    blank[...] = jnp.zeros(blank.shape, F32)


def first_kernel(
    state, extract, send, blank, table, ek, out_d, out_c, out_b, out_a, full, padded, ba, bb, bc, bd, sems
):
    for f in range(4):
        full[pl.ds(f * LANES, NF), pl.ds(0, NQ)] = extract[:, f, :]
    ek[...] = right_parts(full[...], 1)
    pad_state(state[...], padded)
    for c in range(ELEMS // CHUNK):
        traces_of_chunk(padded, ek, table, c)
    copies = gather_sends(send, table, (ba, bb, bc, bd), None, (out_a, out_b, out_c, out_d), sems)
    for copy in copies:
        copy.wait()


def prepare_kernel(
    extract, volume, flux, lift, ocean, wet, sf_face, sf_dest, v2k, l2k, ea, eb, ec, ed, pick, into, v2, l2
):
    place_faces(sf_face, sf_dest, pick, into)
    total = volume[...]
    fl = split(flux[...])
    l2[...] = jnp.zeros(l2.shape, F32)
    v2[...] = jnp.zeros(v2.shape, F32)
    for f in range(4):
        folded = dot3(split(lift[:, f, :]), fl)
        l2[:, pl.ds(f * LANES, NF)] = folded
        total = total + dot3(split(folded), split(extract[:, f, :]))
    v2[:, pl.ds(0, NQ)] = total
    v2k[...] = left_parts(v2[...], 1)
    l2k[...] = left_parts(l2[...], 1)
    _, _, odd_row, odd_col = parities()
    lane = lax.broadcasted_iota(jnp.int32, (TILE, LANES), 1)
    west = wet[:, 0:1].astype(F32)
    east = wet[:, TILE - 1 : TILE].astype(F32)
    north = wet[0:1, :].astype(F32)
    south = wet[TILE - 1 : TILE, :].astype(F32)
    to_c = jnp.zeros((TILE, LANES), F32)
    to_d = jnp.zeros((TILE, LANES), F32)
    rows_a = []
    rows_b = []
    for f in range(3):
        left = ocean[f, :, 0:1] * west
        right = ocean[f, :, TILE - 1 : TILE] * east
        to_c = jnp.where(lane == EDGE_LANE + f, jnp.where(odd_col == 1, left, right), to_c)
        to_d = jnp.where(lane == EDGE_LANE + f, jnp.where(odd_col == 1, right, left), to_d)
        top = ocean[f, 0:1, :] * north
        bottom = ocean[f, TILE - 1 : TILE, :] * south
        for rows, edge in (
            (rows_a, jnp.where(odd_row == 1, top, bottom)),
            (rows_b, jnp.where(odd_row == 1, bottom, top)),
        ):
            rows += [edge[:, t * LANES : (t + 1) * LANES] for t in range(4)]
    spare = [jnp.zeros((EDGE - 12, LANES), F32)]
    ea[...] = jnp.concatenate(rows_a + spare, axis=0)
    eb[...] = jnp.concatenate(rows_b + spare, axis=0)
    ec[...] = to_c
    ed[...] = to_d


def receive(table, recv, sems):
    copies = []
    for i, slot in enumerate(slots()):
        at = pl.multiple_of(POOL + slot * SEND, SEND)
        copy = pltpu.make_async_copy(recv[i].at[pl.ds(0, SEND), :], table.at[pl.ds(at, SEND), :], sems.at[i])
        copy.start()
        copies.append(copy)
    return copies


def zero_absent(table):
    row, col, _, _ = parities()
    for gone, slot in (
        (row == 0, 0), (row == N_ROW - 1, 1), (col == 0, 2), (col == N_COL - 1, 3),
    ):
        @pl.when(gone)
        def _():
            table[pl.ds(POOL + slot * SEND, SEND), :] = jnp.zeros((SEND, LANES), F32)


def gather_part(index, table, near, at):
    for f in range(4):
        for u in range(0, SIZE, 8):
            base = 4 * at + (u // LANES) * (4 * LANES) + f * LANES + u % LANES
            got = [table[pl.ds(index[base + t], 1), :] for t in range(8)]
            near[pl.ds(f * SIZE + u, 8), :] = jnp.concatenate(got, axis=0)


def advance_part(q, near, jac, v2k, l2k, at):
    here = pl.ds(at, SIZE)
    mine = q[:, here]
    inner = dot(v2k[...], right_parts(mine, 0))
    gathered = jnp.concatenate([near[pl.ds(f * SIZE, SIZE), :] for f in range(4)], axis=1)
    lifted = dot(l2k[...], right_parts(gathered, 1), NT)
    return mine[:NQ] + 0.25 * jac[:, here] * (inner - lifted)


def sweep(index, table, near0, near1, work):
    pairs = ELEMS // SIZE // 2
    gather_part(index, table, near0, 0)

    def step(i, carry):
        at = pl.multiple_of(i * (2 * SIZE), 2 * SIZE)
        gather_part(index, table, near1, at + SIZE)
        work(near0, at)
        gather_part(index, table, near0, at + 2 * SIZE)
        work(near1, at + SIZE)
        return carry

    lax.fori_loop(0, pairs - 1, step, 0)
    at = ELEMS - 2 * SIZE
    gather_part(index, table, near1, at + SIZE)
    work(near0, at)
    work(near1, at + SIZE)


def middle_kernel(
    state, jac, ek, v2k, l2k, ea, eb, ec, ed, nbr, send, table_in, in_d, in_c, in_b, in_a,
    new_state, table, out_d, out_c, out_b, out_a,
    padded, near0, near1, ba, bb, bc, bd, sems, out_sems,
):
    arriving = receive(table, (in_a, in_b, in_c, in_d), sems)
    pad_state(state[...], padded)
    for copy in arriving:
        copy.wait()
    zero_absent(table)

    def work(near, at):
        new_state[:, pl.ds(at, SIZE)] = advance_part(padded, near, jac, v2k, l2k, at)

    sweep(nbr, table, near0, near1, work)
    padded[pl.ds(0, NQ), :] = new_state[...]
    for c in range(ELEMS // CHUNK):
        traces_of_chunk(padded, ek, table, c)
    copies = gather_sends(
        send, table, (ba, bb, bc, bd), (ea, eb, ec, ed), (out_a, out_b, out_c, out_d), out_sems
    )
    for copy in copies:
        copy.wait()


def last_kernel(
    state, jac, extract, v2k, l2k, nbr, sf_face, pick, into, sf_row, sf_col, weights, table_in, in_d, in_c, in_b, in_a,
    new_state, table, stay, box_a, box_b,
    padded, near0, near1, new_local, sems, out_sem,
):
    arriving = receive(table, (in_a, in_b, in_c, in_d), sems)
    pad_state(state[...], padded)
    for copy in arriving:
        copy.wait()
    zero_absent(table)

    def work(near, at):
        new_local[:, pl.ds(at, SIZE)] = advance_part(padded, near, jac, v2k, l2k, at)

    sweep(nbr, table, near0, near1, work)
    leaving = pltpu.make_async_copy(new_local, new_state, out_sem)
    leaving.start()
    ops = jnp.concatenate([extract[20:30, f, :] for f in range(4)], axis=0)
    on_faces = dot3(split(ops), split(new_local[...]))
    face = sf_face[...] // ELEMS
    fh, fl = split(on_faces)
    chosen = dot(fh, pick[...]) + dot(fl, pick[...])
    vz = jnp.zeros((10, SF), F32)
    for f in range(4):
        vz = vz + jnp.where(face == f, chosen[f * 10 : (f + 1) * 10, :], 0.0)
    values = weights[0] * vz[0:1]
    for k in range(1, 10):
        values = values + weights[k] * vz[k : k + 1]
    values = jnp.concatenate(
        [values, sf_row[...].astype(F32), sf_col[...].astype(F32), jnp.zeros((6, SF), F32)], axis=0
    )
    vh, vl = split(values)
    box = dot(vh, into[...], NT) + dot(vl, into[...], NT)
    stay[...] = box[:, :GROUP]
    box_a[...] = box[:, GROUP : 2 * GROUP]
    box_b[...] = box[:, 2 * GROUP :]
    leaving.wait()


def place_faces(sf_face, sf_dest, pick, into):
    elem = sf_face[...] % ELEMS
    pick[...] = (lax.broadcasted_iota(jnp.int32, (ELEMS, SF), 0) == elem).astype(BF16)
    row, col, odd_row, odd_col = parities()
    dest = sf_dest[...]
    dr = dest // N_COL - row
    dc = dest % N_COL - col
    to_a = 1 - 2 * odd_row
    to_c = 1 - 2 * odd_col
    group_r = jnp.where(dr == 0, 0, jnp.where(dr == to_a, 1, 2))
    group_c = jnp.where(dc == 0, 0, jnp.where(dc == to_c, 1, 2))
    group = group_r * 3 + group_c
    groups = lax.broadcasted_iota(jnp.int32, (16, SF), 0)
    owners = (groups == group).astype(F32)
    before = (
        lax.broadcasted_iota(jnp.int32, (SF, SF), 0) < lax.broadcasted_iota(jnp.int32, (SF, SF), 1)
    ).astype(BF16)
    ranks = dot(owners.astype(BF16), before)
    rank = jnp.sum(ranks * owners, axis=0, keepdims=True).astype(jnp.int32)
    place = group_r * GROUP + group_c * CAP + rank
    into[...] = (lax.broadcasted_iota(jnp.int32, (3 * GROUP, SF), 0) == place).astype(BF16)


def stencil_kernel(ocean, wet, depth, after, height, speeds, fields):
    wet_f = wet[...].astype(F32)
    for f in range(3):
        fields[f, pl.ds(0, 8), :] = jnp.zeros((8, TILE), F32)
        fields[f, pl.ds(TILE + 8, 8), :] = jnp.zeros((8, TILE), F32)
        fields[f, pl.ds(8, TILE), :] = ocean[f] * wet_f
    rows = 64
    lane = lax.broadcasted_iota(jnp.int32, (rows, TILE), 1)

    def step(i, carry):
        at = pl.multiple_of(i * rows, rows)
        mask = wet[pl.ds(at, rows), :].astype(F32)
        sums, across, along = [], [], []
        for f in range(3):
            big = fields[f, pl.ds(at, rows + 16), :]
            mine = big[8 : 8 + rows]
            up = big[7 : 7 + rows]
            down = big[9 : 9 + rows]
            west = jnp.where(lane == 0, 0.0, pltpu.roll(mine, 1, 1))
            east = jnp.where(lane == TILE - 1, 0.0, pltpu.roll(mine, TILE - 1, 1))
            sums.append(0.25 * ((up + down) + (west + east)))
            across.append(east - west)
            along.append(down - up)
        d = 0.2 * depth[pl.ds(at, rows), :]
        height[pl.ds(at, rows), :] = (sums[0] - 0.2 * (across[1] + along[2])) * mask
        speeds[0, pl.ds(at, rows), :] = (sums[1] - d * across[0]) * mask
        speeds[1, pl.ds(at, rows), :] = (sums[2] - d * along[0]) * mask
        return carry

    lax.fori_loop(0, TILE // rows, step, 0)


def add_edges(height, speeds, wet, depth, ga, gb, gc, gd):
    row, col, odd_row, odd_col = parities()
    gone_b = (row == 0) | (row == N_ROW - 1)
    gone_d = (col == 0) | (col == N_COL - 1)

    def edge_row(got, f):
        return jnp.concatenate([got[pl.ds(4 * f + t, 1), :] for t in range(4)], axis=1)

    from_a = [edge_row(ga, f) for f in range(3)]
    from_b = [jnp.where(gone_b, 0.0, edge_row(gb, f)) for f in range(3)]
    for at, sign, odd in ((0, 1.0, 1), (TILE - 1, -1.0, 0)):
        h, u, v = [jnp.where(odd_row == odd, x, y) for x, y in zip(from_a, from_b)]
        here = pl.ds(at, 1)
        mask = wet[here, :].astype(F32)
        d = (sign * 0.2) * depth[here, :]
        height[here, :] = height[here, :] + mask * (0.25 * h + (sign * 0.2) * v)
        speeds[0, here, :] = speeds[0, here, :] + mask * (0.25 * u)
        speeds[1, here, :] = speeds[1, here, :] + mask * (0.25 * v + d * h)
    lane = lax.broadcasted_iota(jnp.int32, (TILE, LANES), 1)
    from_c = [gc[:, EDGE_LANE + f : EDGE_LANE + f + 1] for f in range(3)]
    from_d = [jnp.where(gone_d, 0.0, gd[:, EDGE_LANE + f : EDGE_LANE + f + 1]) for f in range(3)]
    for at, edge, sign, odd in ((0, 0, 1.0, 1), (TILE - LANES, LANES - 1, -1.0, 0)):
        h, u, v = [jnp.where(odd_col == odd, x, y) for x, y in zip(from_c, from_d)]
        here = pl.ds(at, LANES)
        mask = jnp.where(lane == edge, wet[:, here].astype(F32), 0.0)
        d = (sign * 0.2) * depth[:, here]
        height[:, here] = height[:, here] + mask * (0.25 * h + (sign * 0.2) * u)
        speeds[0, :, here] = speeds[0, :, here] + mask * (0.25 * u + d * h)
        speeds[1, :, here] = speeds[1, :, here] + mask * (0.25 * v)


def uplift_of(data, first=0, columns=TILE):
    total = data.shape[1]
    d_row = lax.broadcasted_iota(jnp.int32, (TILE, total), 0) - data[16:17, :].astype(jnp.int32)
    d_col = lax.broadcasted_iota(jnp.int32, (columns, total), 0) + (first - data[17:18, :].astype(jnp.int32))
    masks = [d_col == b for b in range(4)]
    added = None
    for a in range(4):
        spread = jnp.zeros((columns, total), F32)
        for b in range(4):
            spread = jnp.where(masks[b], data[4 * a + b : 4 * a + b + 1, :], spread)
        pick = (d_row == a).astype(BF16)
        part = dot(jnp.concatenate([pick, pick], axis=1), jnp.concatenate(split(spread), axis=1), NT)
        added = part if added is None else added + part
    return added


def side_by_side(blocks, first):
    half = lax.broadcasted_iota(jnp.int32, (24, LANES), 1) < CAP

    def at_lane(x, lane):
        if x is None:
            return jnp.zeros((24, LANES), F32)
        return x if lane == first else pltpu.roll(x, CAP, 1)

    pairs = [(blocks[i], blocks[i + 1] if i + 1 < len(blocks) else None) for i in range(0, len(blocks), 2)]
    return jnp.concatenate([jnp.where(half, at_lane(x, 0), at_lane(y, CAP)) for x, y in pairs], axis=1)


def finish_edges_kernel(
    stay, wet, depth, height_in, speeds_in, in_d, in_c, in_b, in_a, height, speeds, ga, gb, gc, gd, sems,
):
    arriving = [
        pltpu.make_async_copy(in_a.at[pl.ds(SEND, EDGE), :], ga, sems.at[0]),
        pltpu.make_async_copy(in_b.at[pl.ds(SEND, EDGE), :], gb, sems.at[1]),
        pltpu.make_async_copy(in_c.at[pl.ds(0, SEND), :], gc, sems.at[2]),
        pltpu.make_async_copy(in_d.at[pl.ds(0, SEND), :], gd, sems.at[3]),
    ]
    for copy in arriving:
        copy.start()
    for copy in arriving:
        copy.wait()
    add_edges(height, speeds, wet, depth, ga, gb, gc, gd)
    added = uplift_of(side_by_side([stay[:, :LANES]], 0))
    height[...] = height[...] + added * wet[...].astype(F32)


def uplift_own_kernel(got_b, got_a, wet, height_in, speeds, height, out, out_sem):
    leaving = pltpu.make_async_copy(speeds, out.at[pl.ds(1, 2)], out_sem)
    leaving.start()
    added = uplift_of(side_by_side([got_b[:, :LANES], got_a[:, :LANES]], 0))
    height[...] = height[...] + added * wet[...].astype(F32)
    leaving.wait()


def uplift_far_kernel(got_d, got_c, wet, height, whole, out, plane, sems):
    half = lax.broadcasted_iota(jnp.int32, (24, LANES), 1) < CAP
    data = jnp.concatenate(
        [jnp.where(half, got_d[pl.ds(24 * g, 24), :], got_c[pl.ds(24 * g, 24), :]) for g in range(3)], axis=1
    )
    size = TILE // 2
    copies = []
    for part in range(2):
        here = pl.ds(part * size, size)
        added = uplift_of(data, part * size, size)
        plane[:, here] = height[:, here] + added * wet[:, here].astype(F32)
        copy = pltpu.make_async_copy(plane.at[:, here], out.at[0, :, here], sems.at[part])
        copy.start()
        copies.append(copy)
    for copy in copies:
        copy.wait()


def exchange(a, b, c, d):
    d = lax.ppermute(d, BOTH, PAIR_D)
    c = lax.ppermute(c, BOTH, PAIR_C)
    b = lax.ppermute(b, BOTH, PAIR_B)
    a = lax.ppermute(a, BOTH, PAIR_A)
    return d, c, b, a


def stored_order(index):
    return index.reshape(4, -1, LANES).transpose(1, 0, 2).reshape(-1)


def body(
    state, neighbours, send_faces, jacobian, face_extract, volume_op, flux_matrix, lift_op,
    sf_face, sf_dest, sf_row, sf_col, sf_weights, ocean, depth, wet,
):
    nbr = stored_order(neighbours)
    send = stored_order(send_faces)
    jac = jacobian.reshape(1, ELEMS)
    extract = face_extract.transpose(1, 0, 2)
    weights = sf_weights.transpose(1, 0, 2)
    dma = pltpu.SemaphoreType.DMA
    short = (SEND, LANES)
    tall = (SEND + EDGE, LANES)
    table_o = ((WHOLE, LANES), F32, VMEM)
    padded = pltpu.VMEM((KP, ELEMS), F32)
    near = [pltpu.VMEM((4 * SIZE, LANES), F32)] * 2

    blank_o = ((4 * LANES, KP), F32, VMEM)
    (blank,) = call(blank_kernel, "blank", [], [blank_o], flops=10**10)()
    table, ek, sd, sc, sb, sa, _ = call(
        first_kernel, "traces_first", [VMEM, VMEM, SMEM, VMEM],
        [table_o, ((4 * LANES, 3 * KP), BF16, VMEM)] + [(short, F32, ANY)] * 4 + [blank_o],
        [padded] + [pltpu.VMEM(short, F32)] * 4 + [dma((4,))], aliases={3: 6}, flops=10**10,
    )(state, extract, send, blank)
    recv = exchange(sa, sb, sc, sd)
    v2k, l2k, ea, eb, ec, ed, pick, into = call(
        prepare_kernel, "prepare", [VMEM] * 8,
        [((NQ, 3 * KP), BF16, VMEM), ((NQ, 12 * LANES), BF16, VMEM)]
        + [((EDGE, LANES), F32, VMEM)] * 2 + [(short, F32, VMEM)] * 2
        + [((ELEMS, SF), BF16, VMEM), ((3 * GROUP, SF), BF16, VMEM)],
        [pltpu.VMEM((NQ, KP), F32), pltpu.VMEM((NQ, 4 * LANES), F32)], flops=5 * 10**9,
    )(extract, volume_op, flux_matrix, lift_op, ocean, wet, sf_face.reshape(1, SF), sf_dest.reshape(1, SF))
    state, table, sd, sc, sb, sa = call(
        middle_kernel, "step_first", [VMEM] * 9 + [SMEM] * 2 + [VMEM] + [ANY] * 4,
        [((NQ, ELEMS), F32, VMEM), table_o] + [(tall, F32, ANY)] * 4,
        [padded] + near + [pltpu.VMEM(tall, F32)] * 4 + [dma((4,)), dma((4,))],
        aliases={11: 1},
    )(state, jac, ek, v2k, l2k, ea, eb, ec, ed, nbr, send, table, *recv)
    recv = exchange(sa, sb, sc, sd)
    height, speeds = call(
        stencil_kernel, "stencil", [VMEM] * 4,
        [
            ((TILE, TILE), F32, VMEM), ((2, TILE, TILE), F32, VMEM),
        ],
        [pltpu.VMEM((3, TILE + 16, TILE), F32)], flops=10**9,
    )(ocean, wet, depth, state[:8, :LANES])
    box_o = ((24, GROUP), F32, VMEM)
    state, _, stay, box_a, box_b = call(
        last_kernel, "step_last", [VMEM] * 5 + [SMEM] + [VMEM] * 7 + [ANY] * 4,
        [((NQ, ELEMS), F32, ANY), table_o, box_o, box_o, box_o],
        [padded] + near + [pltpu.VMEM((NQ, ELEMS), F32), dma((4,)), dma(())],
        aliases={12: 1},
    )(
        state, jac, extract, v2k, l2k, nbr, sf_face.reshape(1, SF), pick, into,
        sf_row.reshape(1, SF), sf_col.reshape(1, SF), weights, table, *recv,
    )
    got_b = lax.ppermute(box_b, BOTH, PAIR_B_SMALL)
    got_a = lax.ppermute(box_a, BOTH, PAIR_A)
    plane_o = ((TILE, TILE), F32, VMEM)
    height, speeds = call(
        finish_edges_kernel, "finish_edges", [VMEM] * 5 + [ANY] * 4,
        [plane_o, ((2, TILE, TILE), F32, VMEM)],
        [pltpu.VMEM((EDGE, LANES), F32)] * 2 + [pltpu.VMEM(short, F32)] * 2 + [dma((4,))],
        aliases={3: 0, 4: 1}, flops=2 * 10**9,
    )(stay, wet, depth, height, speeds, *recv)
    mine = jnp.concatenate([stay, got_b, got_a], axis=0)
    got_d = lax.ppermute(mine[:, LANES:], BOTH, PAIR_D)
    got_c = lax.ppermute(jnp.pad(mine[:, :LANES], ((0, 8), (0, 0))), BOTH, PAIR_C)
    height, ocean_out = call(
        uplift_own_kernel, "uplift_own", [VMEM] * 5, [plane_o, ((3, TILE, TILE), F32, ANY)], [dma(())],
        aliases={3: 0}, flops=10**9,
    )(got_b, got_a, wet, height, speeds)
    (ocean_out,) = call(
        uplift_far_kernel, "uplift_far", [VMEM] * 4 + [ANY], [((3, TILE, TILE), F32, ANY)],
        [pltpu.VMEM((TILE, TILE), F32), dma((2,))], aliases={4: 0}, flops=3 * 10**9,
    )(got_d, got_c, wet, height, ocean_out)
    return state, ocean_out


def solution(mesh):
    both = ("row", "col")
    return jax.shard_map(
        body,
        mesh=mesh,
        in_specs=(
            P(None, both), P(None, both), P(None, both), P(both), P(), P(), P(), P(),
            P(both), P(both, None), P(both), P(both), P(None, None, both),
            P(None, "row", "col"), P("row", "col"), P("row", "col"),
        ),
        out_specs=(P(None, both), P(None, "row", "col")),
        check_vma=False,
    )
```
